32 devices in a mesh: section: 16 (over z, y, x), tp: 2 (over core).
Axes of the slice: x: 2, y: 2, z: 4, core: 2. Of those that a mesh axis runs over, the one named last changes fastest.
Arguments:
- prefill_hidden: bfloat16 [4096, 8192], P('section', 'tp'), may hold values from -180 to 180
- norm_gain: float32 [8192], replicated, may hold values from 0.25 to 1.75
- key_weight: bfloat16 [8192, 1024], P(None, 'tp'), may hold values from -0.0625 to 0.0625
- value_weight: bfloat16 [8192, 1024], P(None, 'tp'), may hold values from -0.0625 to 0.0625
- prefill_query: bfloat16 [4096, 8192], P('section', 'tp'), may hold values from -102 to 102
- resident_keys: bfloat16 [4096, 16, 1024], P('section', None, 'tp'), may hold values from -6 to 6
- resident_values: bfloat16 [4096, 16, 1024], P('section', None, 'tp'), may hold values from -6 to 6
- decode_query: bfloat16 [256, 8192], P('section', 'tp'), may hold values from -102 to 102
- page_owner: int32 [256], P('section'), may hold values from 0 to 15, as said below
- block_table: int32 [256, 62], P('section'), may hold values from 0 to 287, as said below
- context_len: int32 [256], P('section'), may hold values from 1 to 992, as said below
Outputs:
- prefill_attention: bfloat16 [4096, 8192], P('section', 'tp')
- decode_attention: bfloat16 [256, 8192], P('section', 'tp')
The draws below stay inside these ranges and needn't reach their ends.
Inputs may be any that keep to these rules, and one draw needn't show every extreme that they name: `page_owner`: the 16 pages of each section device go to 8 different owners, exactly 2 pages to each; one owner receives pages from every section device. `block_table`: row entries name first the row's resident pages (below 256), then 256 + page_slot for at most 2 pages sent to the row's owner; every page sent to an owner is named by exactly one of its rows; entries after a row's pages are 0. `context_len`: A row's last visible token lies in the last page its table names.
All inputs are finite; a program needn't handle non-finite values.
Results may differ from the reference program's by a relative error of at most 0.011.
Values may be sent and summed in bfloat16 or wider, within the bound.
No kernel may reach another device: no remote copies, remote signals or barrier semaphores. Data moves between devices by JAX's collectives and lax.ppermute only.
A program may use at most 256 MiB of HBM per device.

```python
import math
import jax
import jax.numpy as jnp
from jax import lax

D = 8192
HQ = 64
KVH = 8
HD = 128
PAGE = 16
CAP = 2
RES_ROW = 60
B_DEV = 16
SEQ = 4096
PAGES_DEV = 16
INC = 32
INC_ROW = 2
MAXP = 62
POOL = 256
ROWS = 256
N_SECTION = 16


def routing_plan(key):
    plan_keys = jax.random.split(jax.random.fold_in(key, 7101), 8)
    owner_ids = jnp.arange(N_SECTION, dtype=jnp.int32)
    picks_each = PAGES_DEV // CAP
    hottest = jax.random.randint(plan_keys[0], (), 0, N_SECTION)
    ranking = jnp.argsort(jax.random.permutation(plan_keys[1], N_SECTION), stable=True).astype(jnp.int32)
    noise = jax.random.randint(plan_keys[2], (N_SECTION, N_SECTION), 0, 2 * N_SECTION)
    favour = 3 * (N_SECTION - ranking)[None, :]
    favour = favour + 100000 * (owner_ids[None, :] == hottest).astype(jnp.int32)
    favour = favour + 50000 * (owner_ids[None, :] == owner_ids[:, None]).astype(jnp.int32)
    priority = (noise + favour) * N_SECTION + owner_ids[None, :]
    chosen = lax.top_k(priority, picks_each)[1].astype(jnp.int32)
    page_keys = jax.random.split(plan_keys[3], N_SECTION)
    shuffled = jax.vmap(lambda one_key: jax.random.permutation(one_key, PAGES_DEV))(page_keys).astype(jnp.int32)
    owners = jnp.take_along_axis(chosen, shuffled // CAP, axis=1)
    picked = jnp.sum((chosen[:, :, None] == owner_ids[None, None, :]).astype(jnp.int32), axis=1)
    return (owners, picked, hottest, plan_keys)


def decode_plan(key):
    owners, picked, hottest, plan_keys = routing_plan(key)
    owner_ids = jnp.arange(N_SECTION, dtype=jnp.int32)
    row_ids = jnp.arange(B_DEV, dtype=jnp.int32)
    filled = jnp.sum(picked, axis=0) * CAP
    source_order = jnp.argsort(1 - jnp.transpose(picked), axis=1, stable=True).astype(jnp.int32)
    entry_index = row_ids[:, None] + B_DEV * jnp.arange(INC_ROW, dtype=jnp.int32)[None, :]
    source_of = source_order[:, jnp.minimum(entry_index // CAP, N_SECTION - 1)]
    slot_of = source_of * CAP + (entry_index % CAP)[None, :, :]
    live_entry = entry_index[None, :, :] < filled[:, None, None]
    incoming_count = jnp.sum(live_entry.astype(jnp.int32), axis=2)
    hot_row = (owner_ids[:, None] == hottest) & (row_ids[None, :] == 0)
    resident_count = jnp.where(hot_row, RES_ROW, jax.random.randint(plan_keys[4], (N_SECTION, B_DEV), 1, RES_ROW + 1))
    resident_pick = jax.random.randint(plan_keys[5], (N_SECTION, B_DEV, MAXP), 0, POOL)
    column_ids = jnp.arange(MAXP, dtype=jnp.int32)[None, None, :]
    incoming_pos = column_ids - resident_count[:, :, None]
    incoming_slot = jnp.take_along_axis(slot_of, jnp.clip(incoming_pos, 0, INC_ROW - 1), axis=2)
    table_rows = jnp.where(column_ids < resident_count[:, :, None], resident_pick, jnp.where(incoming_pos < incoming_count[:, :, None], POOL + incoming_slot, 0))
    trimmed = jnp.where(hot_row, 0, jax.random.randint(plan_keys[6], (N_SECTION, B_DEV), 0, PAGE))
    row_length = PAGE * (resident_count + incoming_count) - trimmed
    return (table_rows.reshape(N_SECTION * B_DEV, MAXP).astype(jnp.int32), row_length.reshape(N_SECTION * B_DEV).astype(jnp.int32))


def draw_page_owner(key, part):
    return routing_plan(key)[0].reshape(N_SECTION * PAGES_DEV).astype(jnp.int32)


def draw_block_table(key, part):
    return decode_plan(key)[0]


def draw_context_len(key, part):
    return decode_plan(key)[1]


def query_values(key, salt, row_count):
    draw_keys = jax.random.split(jax.random.fold_in(key, salt), 1)
    return jnp.clip(2.5 * jax.random.normal(draw_keys[0], (row_count, HQ * HD), jnp.float32), -12.0, 12.0)


def draw_prefill_query(key, part):
    return query_values(key, 4409, SEQ).astype(jnp.bfloat16)


def draw_decode_query(key, part):
    return query_values(key, 5519, ROWS).astype(jnp.bfloat16)


def draw_prefill_hidden(key, part):
    draw_keys = jax.random.split(jax.random.fold_in(key, 2203), 3)
    row_scale = jnp.exp(jax.random.uniform(draw_keys[1], (SEQ, 1), jnp.float32, 0.0, math.log(10.0)))
    column_scale = jnp.exp(jax.random.uniform(draw_keys[2], (1, D), jnp.float32, math.log(0.3), math.log(3.0)))
    base_values = jnp.clip(jax.random.normal(draw_keys[0], (SEQ, D), jnp.float32), -6.0, 6.0)
    return (base_values * row_scale * column_scale).astype(jnp.bfloat16)


def levels(rng, dims, shards, smallest, largest):
    def one(position, shards_of):
        heights = jax.random.uniform(jax.random.fold_in(jax.random.fold_in(rng, 6), position), (shards_of,), jnp.float32, smallest / len(shards), largest / len(shards))
        return jnp.repeat(jnp.exp(heights), dims[position] // shards_of).reshape((-1,) + (1,) * (len(dims) - position - 1))

    level = one(*shards[0])
    for cut in shards[1:]:
        level = level * one(*cut)
    return level


def gaussian(stream_key, shape, width, most, cuts=(), held_as=jnp.bfloat16):
    result = width * jax.random.normal(stream_key, shape, jnp.float32)
    if cuts:
        result = result * levels(stream_key, shape, cuts, -0.22, 0.18)
    return jnp.clip(result, -most, most).astype(held_as)


def setup_inputs(seed: int = 0) -> dict:
    seeds = jax.random.split(jax.random.key(seed), 12)
    prefill_hidden = draw_prefill_hidden(jax.random.fold_in(seeds[11], 71), 0)
    norm_gain = jnp.clip(1.0 + 0.15 * jax.random.normal(seeds[1], (D,), jnp.float32), 0.25, 1.75)
    key_weight = gaussian(seeds[2], (D, KVH * HD), D ** -0.5, 0.0625, ((1, 2),))
    value_weight = gaussian(seeds[3], (D, KVH * HD), D ** -0.5, 0.0625, ((1, 2),))
    prefill_query = draw_prefill_query(jax.random.fold_in(seeds[11], 71), 0)
    resident_keys = gaussian(seeds[5], (N_SECTION * POOL, PAGE, KVH * HD), 1.0, 6.0, ((0, 16), (2, 2)))
    resident_values = gaussian(seeds[6], (N_SECTION * POOL, PAGE, KVH * HD), 1.0, 6.0, ((0, 16), (2, 2)))
    decode_query = draw_decode_query(jax.random.fold_in(seeds[11], 71), 0)
    page_owner = draw_page_owner(jax.random.fold_in(seeds[11], 71), 0)
    block_table = draw_block_table(jax.random.fold_in(seeds[11], 71), 0)
    context_len = draw_context_len(jax.random.fold_in(seeds[11], 71), 0)
    return {"prefill_hidden": prefill_hidden, "norm_gain": norm_gain, "key_weight": key_weight, "value_weight": value_weight, "prefill_query": prefill_query, "resident_keys": resident_keys, "resident_values": resident_values, "decode_query": decode_query, "page_owner": page_owner, "block_table": block_table, "context_len": context_len}


NORM_EPSILON = 1e-05
ROPE_THETA = 500000.0

def rotate_keys(raw_keys, positions):
    head_width = raw_keys.shape[-1]
    half_width = head_width // 2
    frequency = jnp.exp(jnp.arange(half_width, dtype=jnp.float32) * (-2.0 * math.log(ROPE_THETA) / head_width))
    angles = positions.astype(jnp.float32)[:, None] * frequency[None, :]
    cosine = jnp.cos(angles)[:, None, :]
    sine_part = jnp.sin(angles)[:, None, :]
    first_half = raw_keys[..., :half_width]
    second_half = raw_keys[..., half_width:]
    return jnp.concatenate([first_half * cosine - second_half * sine_part, second_half * cosine + first_half * sine_part], axis=-1)

def reference(prefill_hidden, norm_gain, key_weight, value_weight, prefill_query, resident_keys, resident_values, decode_query, page_owner, block_table, context_len):
    seq_rows = prefill_hidden.shape[0]
    key_width = KVH * HD
    group_size = HQ // KVH
    score_scale = 1.0 / math.sqrt(HD)
    hidden_f32 = prefill_hidden.astype(jnp.float32)
    inverse_rms = lax.rsqrt(lax.optimization_barrier(jnp.mean(hidden_f32 * hidden_f32, axis=1, keepdims=True)) + NORM_EPSILON)
    normed = (hidden_f32 * inverse_rms * norm_gain.astype(jnp.float32)).astype(jnp.bfloat16)
    raw_keys = jnp.dot(normed, key_weight, preferred_element_type=jnp.float32)
    value_rows = jnp.dot(normed, value_weight, preferred_element_type=jnp.float32).astype(jnp.bfloat16)
    positions = jnp.arange(seq_rows, dtype=jnp.int32)
    key_rows = rotate_keys(raw_keys.reshape(seq_rows, KVH, HD), positions).reshape(seq_rows, key_width).astype(jnp.bfloat16)
    block_rows = math.gcd(seq_rows, 128)
    key_f32 = key_rows.astype(jnp.float32).reshape(seq_rows, KVH, HD)
    value_f32 = value_rows.astype(jnp.float32).reshape(seq_rows, KVH, HD)
    query_blocks = prefill_query.reshape(seq_rows // block_rows, block_rows, KVH, group_size, HD)
    block_starts = jnp.arange(seq_rows // block_rows, dtype=jnp.int32) * block_rows

    def prefill_block(inputs):
        query_block, first_row = inputs
        query_pos = first_row + jnp.arange(block_rows, dtype=jnp.int32)
        scores = jnp.einsum('tkgd,rkd->kgtr', query_block.astype(jnp.float32), key_f32) * score_scale
        visible = positions[None, :] <= query_pos[:, None]
        scores = jnp.where(visible, scores, -jnp.inf)
        row_max = lax.optimization_barrier(jnp.max(scores, axis=-1, keepdims=True))
        weights = jnp.exp(scores - row_max)
        row_sum = lax.optimization_barrier(jnp.sum(weights, axis=-1, keepdims=True))
        rounded = lax.optimization_barrier(weights.astype(jnp.bfloat16)).astype(jnp.float32)
        attended = jnp.einsum('kgtr,rkd->kgtd', rounded, value_f32) / row_sum
        return jnp.transpose(attended, (2, 0, 1, 3)).reshape(block_rows, HQ * HD).astype(jnp.bfloat16)
    prefill_attention = lax.map(prefill_block, (query_blocks, block_starts)).reshape(seq_rows, HQ * HD)
    sections = N_SECTION
    pages_total = seq_rows // PAGE
    pages_each = pages_total // sections
    page_data = jnp.concatenate([key_rows, value_rows], axis=1).reshape(pages_total, PAGE, 2 * key_width)
    owners = page_owner.reshape(sections, pages_each)
    page_index = jnp.arange(pages_each, dtype=jnp.int32)
    earlier = (owners[:, :, None] == owners[:, None, :]) & (page_index[None, None, :] < page_index[None, :, None])
    page_rank = lax.optimization_barrier(jnp.sum(earlier.astype(jnp.int32), axis=2))
    source_section = jnp.arange(sections, dtype=jnp.int32)[:, None]
    target = (owners * INC + source_section * CAP + page_rank).reshape(pages_total).astype(jnp.int32)
    incoming = jnp.zeros((sections * INC, PAGE, 2 * key_width), jnp.bfloat16).at[target].set(page_data)
    incoming = incoming.reshape(sections, INC, PAGE, 2 * key_width)
    cache_keys = jnp.concatenate([resident_keys.reshape(sections, POOL, PAGE, key_width), incoming[..., :key_width]], axis=1)
    cache_values = jnp.concatenate([resident_values.reshape(sections, POOL, PAGE, key_width), incoming[..., key_width:]], axis=1)
    tables = block_table.reshape(sections, B_DEV, MAXP)
    lengths = context_len.reshape(sections, B_DEV)
    queries = decode_query.reshape(sections, B_DEV, KVH, group_size, HD)
    key_span = MAXP * PAGE

    def decode_group(inputs):
        group_keys, group_values, table_rows, length_rows, query_rows = inputs
        gathered_keys = group_keys[table_rows].reshape(B_DEV, key_span, KVH, HD).astype(jnp.float32)
        gathered_values = group_values[table_rows].reshape(B_DEV, key_span, KVH, HD).astype(jnp.float32)
        scores = jnp.einsum('bkgd,blkd->bkgl', query_rows.astype(jnp.float32), gathered_keys) * score_scale
        visible = (jnp.arange(key_span, dtype=jnp.int32)[None, :] < length_rows[:, None])[:, None, None, :]
        scores = jnp.where(visible, scores, -jnp.inf)
        row_max = lax.optimization_barrier(jnp.max(scores, axis=-1, keepdims=True))
        weights = jnp.exp(scores - row_max)
        row_sum = lax.optimization_barrier(jnp.sum(weights, axis=-1, keepdims=True))
        rounded = lax.optimization_barrier(weights.astype(jnp.bfloat16)).astype(jnp.float32)
        attended = jnp.einsum('bkgl,blkd->bkgd', rounded, gathered_values) / row_sum
        return attended.reshape(B_DEV, HQ * HD).astype(jnp.bfloat16)
    decode_attention = lax.map(decode_group, (cache_keys, cache_values, tables, lengths, queries)).reshape(ROWS, HQ * HD)
    return (prefill_attention, decode_attention)
```

```python
import functools
import math

import jax
import jax.numpy as jnp
from jax import lax
from jax.experimental import pallas as pl
from jax.experimental.pallas import tpu as pltpu
from jax.sharding import PartitionSpec as P

HD = 128
PAGE = 16
CAP = 2
NORM_EPSILON = 1e-05
ROPE_THETA = 500000.0
LOW = -1e30
EXP2_SCALE = math.log2(math.e) / math.sqrt(HD)
VMEM_BYTES = 56 * 1024 * 1024
NT = (((1,), (1,)), ((), ()))


def params(**kwargs):
    return pltpu.CompilerParams(vmem_limit_bytes=VMEM_BYTES, **kwargs)


def project_kernel(n_parts, chunk, order_ref, *refs):
    parts = refs[:n_parts]
    gain_ref, key_ref, value_ref, cos_ref, sin_ref, out_ref, inv_ref, total_ref = refs[n_parts:]
    step = pl.program_id(0)
    part_width = parts[0].shape[1]
    per_part = part_width // chunk
    width = part_width * n_parts
    key_width = key_ref.shape[1]

    @pl.when(step == 0)
    def _():
        squares = jnp.zeros((parts[0].shape[0], 1), jnp.float32)
        for part in parts:
            for first in range(0, part_width, chunk):
                piece = part[:, first : first + chunk].astype(jnp.float32)
                squares += jnp.sum(piece * piece, axis=1, keepdims=True)
        inverse = lax.rsqrt(squares * (1.0 / width) + NORM_EPSILON)
        inv_ref[...] = jnp.broadcast_to(inverse, inv_ref.shape)
        total_ref[...] = jnp.zeros_like(total_ref)

    for index, part in enumerate(parts):

        @pl.when(step // per_part == index)
        def _(part=part):
            first = pl.multiple_of((step % per_part) * chunk, chunk)
            piece = part[:, pl.ds(first, chunk)].astype(jnp.float32)
            normed = (piece * inv_ref[:, :1] * gain_ref[...]).astype(jnp.bfloat16)
            total_ref[:, :key_width] += jnp.dot(
                normed, key_ref[...], preferred_element_type=jnp.float32
            )
            total_ref[:, key_width:] += jnp.dot(
                normed, value_ref[...], preferred_element_type=jnp.float32
            )

    @pl.when(step == n_parts * per_part - 1)
    def _():
        for head in range(key_width // HD):
            cut = slice(head * HD, (head + 1) * HD)
            raw = total_ref[:, cut]
            turned = raw * cos_ref[...] + pltpu.roll(raw, HD // 2, 1) * sin_ref[...]
            out_ref[:, cut] = turned.astype(jnp.bfloat16)
        out_ref[:, key_width:] = total_ref[:, key_width:].astype(jnp.bfloat16)


def project(parts, order, norm_gain, key_weight, value_weight, cosine, sine):
    rows, part_width = parts[0].shape
    n_parts = len(parts)
    key_width = key_weight.shape[1]
    chunk = math.gcd(part_width, 1024)
    per_part = part_width // chunk

    def weight_index(step, order_ref):
        return (order_ref[step // per_part] * per_part + step % per_part, 0)

    def gain_index(step, order_ref):
        return (0, order_ref[step // per_part] * per_part + step % per_part)

    def whole(step, order_ref):
        return (0, 0)

    return pl.pallas_call(
        functools.partial(project_kernel, n_parts, chunk),
        out_shape=jax.ShapeDtypeStruct((rows, 2 * key_width), jnp.bfloat16),
        grid_spec=pltpu.PrefetchScalarGridSpec(
            num_scalar_prefetch=1,
            grid=(n_parts * per_part,),
            in_specs=[pl.BlockSpec((rows, part_width), whole)] * n_parts
            + [
                pl.BlockSpec((1, chunk), gain_index),
                pl.BlockSpec((chunk, key_width), weight_index),
                pl.BlockSpec((chunk, key_width), weight_index),
                pl.BlockSpec((rows, HD), whole),
                pl.BlockSpec((rows, HD), whole),
            ],
            out_specs=pl.BlockSpec((rows, 2 * key_width), whole),
            scratch_shapes=[
                pltpu.VMEM((rows, HD), jnp.float32),
                pltpu.VMEM((rows, 2 * key_width), jnp.float32),
            ],
        ),
        compiler_params=params(),
        cost_estimate=pl.CostEstimate(
            flops=4 * rows * key_width * part_width * n_parts,
            bytes_accessed=4 * key_width * part_width * n_parts,
            transcendentals=0,
        ),
        name="project",
    )(order, *parts, norm_gain.reshape(1, -1), key_weight, value_weight, cosine, sine)


def stack_heads(ref, group):
    return jnp.concatenate([ref[:, h * HD : (h + 1) * HD] for h in range(group)], axis=0)


def with_ones(values):
    return jnp.concatenate([values, jnp.ones_like(values)], axis=1)


def join_stats(row_max, row_sum):
    lanes = lax.broadcasted_iota(jnp.int32, (row_max.shape[0], HD), 1)
    return jnp.where(lanes < HD // 2, row_max, row_sum)


def counted_piece(queries, keys, values_ones, counts, old_max):
    scores = lax.dot_general(queries, keys, NT, preferred_element_type=jnp.float32)
    counts = jnp.concatenate([counts] * (queries.shape[0] // counts.shape[0]), axis=0)
    scores = jnp.where(counts > 0, scores * EXP2_SCALE, LOW)
    new_max = jnp.maximum(old_max, jnp.max(scores, axis=1, keepdims=True))
    weights = jnp.where(counts > 0, jnp.exp2(scores - new_max) * counts, 0.0)
    product = jnp.dot(
        weights.astype(jnp.bfloat16), values_ones, preferred_element_type=jnp.float32
    )
    return new_max, product


def resident_kernel(group, query_ref, key_ref, value_ref, count_ref, acc_ref, stat_ref):
    queries = stack_heads(query_ref, group)
    rows = queries.shape[0]
    new_max, product = counted_piece(
        queries,
        key_ref[...],
        with_ones(value_ref[...]),
        count_ref[...],
        jnp.full((rows, 1), LOW, jnp.float32),
    )
    acc_ref[0] = product[:, :HD]
    stat_ref[0] = join_stats(new_max, product[:, HD:])


def resident_attention(decode_query, keys, values, counts):
    rows, query_width = decode_query.shape
    pool_rows, key_width = keys.shape
    kv_heads = key_width // HD
    group = query_width // key_width
    state = jax.ShapeDtypeStruct((kv_heads, group * rows, HD), jnp.float32)
    return pl.pallas_call(
        functools.partial(resident_kernel, group),
        out_shape=(state, state),
        grid=(kv_heads,),
        in_specs=[
            pl.BlockSpec((rows, group * HD), lambda g: (0, g)),
            pl.BlockSpec((pool_rows, HD), lambda g: (0, g)),
            pl.BlockSpec((pool_rows, HD), lambda g: (0, g)),
            pl.BlockSpec((rows, pool_rows), lambda g: (0, 0)),
        ],
        out_specs=[pl.BlockSpec((1, group * rows, HD), lambda g: (g, 0, 0))] * 2,
        compiler_params=params(),
        cost_estimate=pl.CostEstimate(
            flops=6 * kv_heads * group * rows * pool_rows * HD,
            bytes_accessed=4 * key_width * pool_rows,
            transcendentals=kv_heads * group * rows * pool_rows,
        ),
        name="resident",
    )(decode_query, keys, values, counts)


def attend_kernel(n_blocks, group, tile_heads, first, final, place_ref, *refs):
    refs = list(refs)

    def take(count):
        taken, refs[:count] = refs[:count], []
        return taken

    query_ref, decode_ref = take(2)
    keys = take(n_blocks)
    values = take(n_blocks)
    counts = take(n_blocks)
    if not first:
        acc_in, stat_in = take(2)
    if final:
        side_acc, side_stat = take(2)
        out_ref, decode_out = take(2)
    else:
        acc_out, stat_out = take(2)
    rows = query_ref.shape[0]
    decode_rows = decode_ref.shape[0]
    own = place_ref[0]
    all_keys = jnp.concatenate([ref[...] for ref in keys], axis=0)
    all_values = jnp.concatenate([with_ones(ref[...]) for ref in values], axis=0)
    seen = [place_ref[1 + b] < own for b in range(n_blocks)]
    tile = tile_heads * rows
    for top in range(0, group * rows, tile):
        heads = range(top // rows, top // rows + tile_heads)
        queries = jnp.concatenate([query_ref[:, h * HD : (h + 1) * HD] for h in heads], axis=0)
        scores = lax.dot_general(queries, all_keys, NT, preferred_element_type=jnp.float32)
        span = scores.shape[1] // n_blocks
        pieces = [scores[:, b * span : (b + 1) * span] for b in range(n_blocks)]
        if first:
            row_of = lax.broadcasted_iota(jnp.int32, (rows, span), 0)
            row_of = jnp.concatenate([row_of] * tile_heads, axis=0)
            column_of = lax.broadcasted_iota(jnp.int32, (tile, span), 1)
            pieces[0] = jnp.where(column_of <= row_of, pieces[0], LOW)
            new_max = jnp.max(pieces[0], axis=1, keepdims=True) * EXP2_SCALE
        else:
            old_max = stat_in[0, top : top + tile, :1]
            new_max = old_max
        for b in range(1 if first else 0, n_blocks):
            highest = jnp.max(pieces[b], axis=1, keepdims=True) * EXP2_SCALE
            new_max = jnp.maximum(new_max, jnp.where(seen[b], highest, LOW))
        weights = []
        for b in range(n_blocks):
            shift = new_max
            if not (first and b == 0):
                shift = new_max + jnp.where(seen[b], 0.0, -LOW)
            weights.append(jnp.exp2(pieces[b] * EXP2_SCALE - shift).astype(jnp.bfloat16))
        product = jnp.dot(
            jnp.concatenate(weights, axis=1), all_values, preferred_element_type=jnp.float32
        )
        acc, total = product[:, :HD], product[:, HD:]
        if not first:
            fade = jnp.exp2(old_max - new_max)
            acc += acc_in[0, top : top + tile, :] * fade
            total += stat_in[0, top : top + tile, HD // 2 : HD // 2 + 1] * fade
        if final:
            result = (acc / total).astype(jnp.bfloat16)
            for place, h in enumerate(heads):
                out_ref[:, h * HD : (h + 1) * HD] = result[place * rows : (place + 1) * rows]
        else:
            acc_out[0, top : top + tile, :] = acc
            stat_out[0, top : top + tile, :] = join_stats(new_max, total)

    queries = stack_heads(decode_ref, group)
    base = group * rows
    small = group * decode_rows
    if first:
        old_max = jnp.full((small, 1), LOW, jnp.float32)
    else:
        old_max = stat_in[0, base : base + small, :1]
    new_max, product = counted_piece(
        queries,
        all_keys,
        all_values,
        jnp.concatenate([ref[...] for ref in counts], axis=1),
        old_max,
    )
    acc, total = product[:, :HD], product[:, HD:]
    if not first:
        fade = jnp.exp2(old_max - new_max)
        acc += acc_in[0, base : base + small, :] * fade
        total += stat_in[0, base : base + small, HD // 2 : HD // 2 + 1] * fade
    if final:
        side_max = side_stat[0, :, :1]
        side_sum = side_stat[0, :, HD // 2 : HD // 2 + 1]
        top_max = jnp.maximum(new_max, side_max)
        fade, side_fade = jnp.exp2(new_max - top_max), jnp.exp2(side_max - top_max)
        acc = acc * fade + side_acc[0] * side_fade
        total = total * fade + side_sum * side_fade
        result = (acc / total).astype(jnp.bfloat16)
        for h in range(group):
            decode_out[:, h * HD : (h + 1) * HD] = result[h * decode_rows : (h + 1) * decode_rows]
    else:
        acc_out[0, base : base + small, :] = acc
        stat_out[0, base : base + small, :] = join_stats(new_max, total)


def attend(place, query, decode_query, blocks, counts, state, side, kv_heads):
    n_blocks = len(blocks)
    rows, query_width = query.shape
    decode_rows = decode_query.shape[0]
    block_rows = blocks[0].shape[0]
    group = query_width // (kv_heads * HD)
    first, final = state is None, side is not None
    total_rows = group * (rows + decode_rows)
    state_spec = pl.BlockSpec((1, total_rows, HD), lambda g, place_ref: (g, 0, 0))
    side_spec = pl.BlockSpec((1, group * decode_rows, HD), lambda g, place_ref: (g, 0, 0))
    query_spec = pl.BlockSpec((rows, group * HD), lambda g, place_ref: (0, g))
    decode_spec = pl.BlockSpec((decode_rows, group * HD), lambda g, place_ref: (0, g))
    key_spec = pl.BlockSpec((block_rows, HD), lambda g, place_ref: (0, g))
    value_spec = pl.BlockSpec((block_rows, HD), lambda g, place_ref: (0, kv_heads + g))
    count_specs = [
        pl.BlockSpec((decode_rows, block_rows), lambda g, place_ref, b=b: (0, place_ref[1 + b]))
        for b in range(n_blocks)
    ]
    operands = [query, decode_query, *blocks, *blocks, *([counts] * n_blocks)]
    in_specs = [query_spec, decode_spec] + [key_spec] * n_blocks + [value_spec] * n_blocks
    in_specs += count_specs
    if not first:
        operands += list(state)
        in_specs += [state_spec] * 2
    if final:
        operands += list(side)
        in_specs += [side_spec] * 2
        out_shape = (
            jax.ShapeDtypeStruct(query.shape, jnp.bfloat16),
            jax.ShapeDtypeStruct(decode_query.shape, jnp.bfloat16),
        )
        out_specs = [query_spec, decode_spec]
    else:
        out_shape = (jax.ShapeDtypeStruct((kv_heads, total_rows, HD), jnp.float32),) * 2
        out_specs = [state_spec] * 2
    tile_heads = math.gcd(group, 2)
    pairs = kv_heads * total_rows * n_blocks * block_rows
    return pl.pallas_call(
        functools.partial(attend_kernel, n_blocks, group, tile_heads, first, final),
        out_shape=out_shape,
        grid_spec=pltpu.PrefetchScalarGridSpec(
            num_scalar_prefetch=1, grid=(kv_heads,), in_specs=in_specs, out_specs=out_specs
        ),
        compiler_params=params(),
        cost_estimate=pl.CostEstimate(
            flops=6 * pairs * HD,
            bytes_accessed=12 * kv_heads * total_rows * HD,
            transcendentals=pairs,
        ),
        name="attend",
    )(place, *operands)


def table_counts(block_table, context_len, cache_pages):
    entries = jnp.arange(block_table.shape[1], dtype=jnp.int32)[None, :]
    length = context_len[:, None]
    whole = (entries + 1) * PAGE <= length
    cut = (entries * PAGE < length) & jnp.logical_not(whole)
    same = block_table[:, :, None] == cache_pages[None, None, :]
    whole_count = jnp.sum((same & whole[:, :, None]).astype(jnp.float32), axis=1)
    cut_count = jnp.sum((same & cut[:, :, None]).astype(jnp.float32), axis=1)
    return whole_count, cut_count


def token_counts(whole_count, cut_count, context_len):
    rows, pages = whole_count.shape
    page_of = jnp.arange(pages * PAGE, dtype=jnp.int32) // PAGE
    spread = (jnp.arange(pages, dtype=jnp.int32)[:, None] == page_of[None, :]).astype(jnp.bfloat16)
    stacked = jnp.concatenate([whole_count, cut_count], axis=0).astype(jnp.bfloat16)
    tokens = jnp.dot(stacked, spread, preferred_element_type=jnp.float32)
    place = jnp.arange(pages * PAGE, dtype=jnp.int32)[None, :] % PAGE
    kept = place < (context_len % PAGE)[:, None]
    return tokens[:rows] + jnp.where(kept, tokens[rows:], 0.0)


def incoming_pages(page_owner, section_count):
    pages = page_owner.shape[0]
    page_index = jnp.arange(pages, dtype=jnp.int32)
    earlier = (page_owner[:, None] == page_owner[None, :]) & (
        page_index[None, :] < page_index[:, None]
    )
    rank = jnp.sum(earlier.astype(jnp.int32), axis=1)
    owners = jnp.arange(section_count, dtype=jnp.int32)
    slots = jnp.arange(CAP, dtype=jnp.int32)
    match = (page_owner[None, None, :] == owners[:, None, None]) & (
        rank[None, None, :] == slots[None, :, None]
    )
    sent = jnp.sum(jnp.where(match, page_index[None, None, :] + 1, 0), axis=2) - 1
    return lax.all_to_all(sent, "section", split_axis=0, concat_axis=0, tiled=True)


def fence(*arrays):
    return lax.optimization_barrier(arrays)


def gather_rounds(own):
    size_z, size_y, size_x = 4, 2, 2
    here = lax.axis_index("section")
    z, column = here // 4, here % 4

    def index(zz, yy, xx):
        return (zz * size_y + yy) * size_x + xx

    def along_z(pairs):
        return [
            (index(a, yy, xx), index(b, yy, xx))
            for a, b in pairs
            for yy in range(size_y)
            for xx in range(size_x)
        ]

    every = [(zz, yy, xx) for zz in range(size_z) for yy in range(size_y) for xx in range(size_x)]
    swap_x = [(index(zz, yy, xx), index(zz, yy, 1 - xx)) for zz, yy, xx in every]
    swap_y = [(index(zz, yy, xx), index(zz, 1 - yy, xx)) for zz, yy, xx in every]
    ends = along_z([(0, 1), (1, 0), (2, 3), (3, 2)])
    middle = along_z([(1, 2), (2, 1)])
    outward = along_z([(1, 0), (2, 3)])
    inward = along_z([(0, 1), (3, 2)])
    inner = (z == 1) | (z == 2)

    def move(block, pairs):
        return lax.ppermute(block, "section", pairs)

    plane_a = jnp.bitwise_xor(z, 1)
    plane_f = jnp.where(inner, 3 - z, jnp.where(z == 0, 2, 1))
    plane_g = jnp.where(inner, jnp.bitwise_xor(3 - z, 1), 3 - z)

    def at(plane, turn):
        return plane * 4 + jnp.bitwise_xor(column, turn)

    own_x, own_y, a, b = fence(
        move(own, swap_x), move(own, swap_y), move(own, ends), move(own, middle)
    )
    rounds = [[(own, here), (own_x, at(z, 1)), (own_y, at(z, 2)), (a, at(plane_a, 0))]]
    yield rounds[-1]
    own_d, a_y, c, d = fence(
        move(own_y, swap_x), move(a, swap_y), move(b, outward), move(a, middle)
    )
    f = jnp.where(inner, b, c)
    yield [(own_d, at(z, 3)), (a_y, at(plane_a, 2)), (f, at(plane_f, 0))]
    a_x, f_y, e, a_in, b_in = fence(
        move(a, swap_x),
        move(f, swap_y),
        move(d, outward),
        move(own_d, inward),
        move(own_d, middle),
    )
    g = jnp.where(inner, d, e)
    yield [(a_x, at(plane_a, 1)), (f_y, at(plane_f, 2)), (g, at(plane_g, 0))]
    f_x, g_y, c_in, d_in = fence(
        move(f, swap_x), move(g, swap_y), move(b_in, outward), move(a_in, middle)
    )
    f_d = jnp.where(inner, b_in, c_in)
    yield [(f_x, at(plane_f, 1)), (g_y, at(plane_g, 2)), (f_d, at(plane_f, 3))]
    g_x, a_turn, e_in = fence(move(g, swap_x), move(a_x, swap_y), move(d_in, outward))
    a_d = jnp.where(inner, a_in, a_turn)
    g_d = jnp.where(inner, d_in, e_in)
    yield [(g_x, at(plane_g, 1)), (a_d, at(plane_a, 3)), (g_d, at(plane_g, 3))]


def gather_plain(own, section_count):
    rows = own.shape[0]
    gathered = lax.all_gather(own, "section", axis=0, tiled=True)
    step = math.gcd(section_count, 4)
    for top in range(0, section_count, step):
        yield [
            (gathered[s * rows : (s + 1) * rows], jnp.int32(s)) for s in range(top, top + step)
        ]


def per_device(
    prefill_hidden,
    norm_gain,
    key_weight,
    value_weight,
    prefill_query,
    resident_keys,
    resident_values,
    decode_query,
    page_owner,
    block_table,
    context_len,
):
    section_count = lax.axis_size("section")
    tp_count = lax.axis_size("tp")
    section = lax.axis_index("section").astype(jnp.int32)
    tp = lax.axis_index("tp").astype(jnp.int32)
    rows = prefill_hidden.shape[0]
    key_width = key_weight.shape[1]
    kv_heads = key_width // HD
    pool = resident_keys.shape[0]

    if tp_count == 2:
        other = lax.ppermute(prefill_hidden, "tp", [(0, 1), (1, 0)])
        parts, order = [prefill_hidden, other], jnp.stack([tp, 1 - tp])
    else:
        parts = [lax.all_gather(prefill_hidden, "tp", axis=1, tiled=True)]
        order = jnp.zeros((1,), jnp.int32)

    half = HD // 2
    frequency = jnp.exp(jnp.arange(half, dtype=jnp.float32) * (-2.0 * math.log(ROPE_THETA) / HD))
    positions = section * rows + jnp.arange(rows, dtype=jnp.int32)
    angles = positions.astype(jnp.float32)[:, None] * frequency[None, :]
    cosine, sine = jnp.cos(angles), jnp.sin(angles)
    cosine = jnp.concatenate([cosine, cosine], axis=1)
    sine = jnp.concatenate([-sine, sine], axis=1)

    own = project(parts, order, norm_gain, key_weight, value_weight, cosine, sine)

    slot_pages = incoming_pages(page_owner, section_count).reshape(-1)
    resident_ids = jnp.arange(pool, dtype=jnp.int32)
    resident_count = token_counts(
        *table_counts(block_table, context_len, resident_ids), context_len
    )
    side = resident_attention(
        decode_query,
        resident_keys.reshape(pool * PAGE, key_width),
        resident_values.reshape(pool * PAGE, key_width),
        resident_count,
    )
    slot_ids = pool + jnp.arange(section_count * CAP, dtype=jnp.int32)
    slot_whole, slot_cut = table_counts(block_table, context_len, slot_ids)
    pages_here = rows // PAGE
    slot_page = jnp.where(
        slot_pages >= 0,
        jnp.arange(section_count * CAP, dtype=jnp.int32) // CAP * pages_here + slot_pages,
        -1,
    )
    pages_all = jnp.arange(section_count * pages_here, dtype=jnp.int32)
    fills = (slot_page[:, None] == pages_all[None, :]).astype(jnp.float32)
    prompt_count = token_counts(
        jnp.dot(slot_whole, fills, precision=lax.Precision.HIGHEST),
        jnp.dot(slot_cut, fills, precision=lax.Precision.HIGHEST),
        context_len,
    )

    if section_count == 16:
        rounds = gather_rounds(own)
        n_rounds, state = 5, None
        later_count = prompt_count
    else:
        first_place = jnp.stack([section, section])
        state = attend(
            first_place, prefill_query, decode_query, [own], prompt_count, None, None, kv_heads
        )
        rounds = gather_plain(own, section_count)
        n_rounds = section_count // math.gcd(section_count, 4)
        mine = jnp.arange(section_count * rows, dtype=jnp.int32) // rows == section
        later_count = jnp.where(mine[None, :], 0.0, prompt_count)
    for number, arrived in enumerate(rounds):
        place = jnp.stack([section] + [s.astype(jnp.int32) for _, s in arrived])
        state = attend(
            place,
            prefill_query,
            decode_query,
            [block for block, _ in arrived],
            later_count,
            state,
            side if number == n_rounds - 1 else None,
            kv_heads,
        )
    return state


def solution(mesh):
    return jax.shard_map(
        per_device,
        mesh=mesh,
        in_specs=(
            P("section", "tp"),
            P(),
            P(None, "tp"),
            P(None, "tp"),
            P("section", "tp"),
            P("section", None, "tp"),
            P("section", None, "tp"),
            P("section", "tp"),
            P("section"),
            P("section", None),
            P("section"),
        ),
        out_specs=(P("section", "tp"), P("section", "tp")),
        check_vma=False,
    )
```

```python
import functools
import math

import jax
import jax.numpy as jnp
from jax import lax
from jax.experimental import pallas as pl
from jax.experimental.pallas import tpu as pltpu
from jax.sharding import PartitionSpec as P

HD = 128
PAGE = 16
CAP = 2
CUT = 1024
NORM_EPSILON = 1e-05
ROPE_THETA = 500000.0
LOW = -1e30
EXP2_SCALE = math.log2(math.e) / math.sqrt(HD)
VMEM_BYTES = 32 * 1024 * 1024
NT = (((1,), (1,)), ((), ()))


def params(limit=VMEM_BYTES):
    return pltpu.CompilerParams(vmem_limit_bytes=limit)


def stage_kernel(n_arrays, *refs):
    copies = [
        pltpu.make_async_copy(refs[i], refs[n_arrays + i], refs[2 * n_arrays].at[i])
        for i in range(n_arrays)
    ]
    for copy in copies:
        copy.start()
    for copy in copies:
        copy.wait()


def stage(*arrays):
    return pl.pallas_call(
        functools.partial(stage_kernel, len(arrays)),
        out_shape=tuple(jax.ShapeDtypeStruct(a.shape, a.dtype) for a in arrays),
        in_specs=[pl.BlockSpec(memory_space=pl.ANY)] * len(arrays),
        out_specs=[pl.BlockSpec(memory_space=pltpu.VMEM)] * len(arrays),
        scratch_shapes=[pltpu.SemaphoreType.DMA((len(arrays),))],
        compiler_params=params(),
        cost_estimate=pl.CostEstimate(
            flops=0, bytes_accessed=sum(2 * a.size * a.dtype.itemsize for a in arrays), transcendentals=0
        ),
        name="stage",
    )(*arrays)


def project_kernel(n_parts, chunk, order_ref, *refs):
    parts = refs[:n_parts]
    gain_ref, key_ref, value_ref, cos_ref, sin_ref, code_ref, out_ref, total_ref = refs[n_parts:]
    rows, part_width = parts[0].shape
    key_width = key_ref.shape[1]
    codes = code_ref[...]
    out_ref[rows:] = jnp.broadcast_to(codes, (codes.shape[0], 2 * key_width)).astype(jnp.bfloat16)
    squares = jnp.zeros((rows, HD), jnp.float32)
    for part in parts:
        for first in range(0, part_width, HD):
            piece = part[:, first : first + HD].astype(jnp.float32)
            squares += piece * piece
    squares = jnp.sum(squares, axis=1, keepdims=True)
    inverse = lax.rsqrt(squares * (1.0 / (part_width * n_parts)) + NORM_EPSILON)
    for index, part in enumerate(parts):
        base = order_ref[index] * part_width
        for first in range(0, part_width, chunk):
            where = pl.multiple_of(base + first, chunk)
            piece = part[:, first : first + chunk].astype(jnp.float32)
            normed = (piece * inverse * gain_ref[:, pl.ds(where, chunk)]).astype(jnp.bfloat16)
            keys = jnp.dot(
                normed, key_ref[pl.ds(where, chunk)], preferred_element_type=jnp.float32
            )
            values = jnp.dot(
                normed, value_ref[pl.ds(where, chunk)], preferred_element_type=jnp.float32
            )
            if index == 0 and first == 0:
                total_ref[:, :key_width] = keys
                total_ref[:, key_width:] = values
            else:
                total_ref[:, :key_width] += keys
                total_ref[:, key_width:] += values
    for head in range(key_width // HD):
        cut = slice(head * HD, (head + 1) * HD)
        raw = total_ref[:, cut]
        turned = raw * cos_ref[...] + pltpu.roll(raw, HD // 2, 1) * sin_ref[...]
        out_ref[:rows, cut] = turned.astype(jnp.bfloat16)
    out_ref[:rows, key_width:] = total_ref[:, key_width:].astype(jnp.bfloat16)


def project(parts, order, norm_gain, key_weight, value_weight, cosine, sine, codes):
    rows, part_width = parts[0].shape
    n_parts = len(parts)
    key_width = key_weight.shape[1]
    vmem = pl.BlockSpec(memory_space=pltpu.VMEM)
    return pl.pallas_call(
        functools.partial(project_kernel, n_parts, math.gcd(part_width, 1024)),
        out_shape=jax.ShapeDtypeStruct((rows + codes.shape[0], 2 * key_width), jnp.bfloat16),
        in_specs=[pl.BlockSpec(memory_space=pltpu.SMEM)] + [vmem] * (n_parts + 6),
        out_specs=vmem,
        scratch_shapes=[pltpu.VMEM((rows, 2 * key_width), jnp.float32)],
        compiler_params=params(),
        cost_estimate=pl.CostEstimate(
            flops=4 * rows * key_width * part_width * n_parts,
            bytes_accessed=4 * key_width * part_width * n_parts,
            transcendentals=0,
        ),
        name="project",
    )(order, *parts, norm_gain.reshape(1, -1), key_weight, value_weight, cosine, sine, codes)


def stack_heads(ref, group):
    return jnp.concatenate([ref[:, h * HD : (h + 1) * HD] for h in range(group)], axis=0)


def turned_with_ones(values):
    turned = values.T
    return jnp.concatenate([turned, jnp.ones((16, turned.shape[1]), turned.dtype)], axis=0)


def counted_piece(queries, keys, values_ones, counts, old_max):
    scores = lax.dot_general(keys, queries, NT, preferred_element_type=jnp.float32)
    scores = jnp.where(counts > 0, scores * EXP2_SCALE, LOW)
    new_max = jnp.maximum(old_max, jnp.max(scores, axis=0, keepdims=True))
    weights = jnp.where(counts > 0, jnp.exp2(scores - new_max) * counts, 0.0)
    product = jnp.dot(
        values_ones, weights.astype(jnp.bfloat16), preferred_element_type=jnp.float32
    )
    return new_max, product


def store_stats(stat_ref, columns, row_max, row_sum):
    stat_ref[0, 0:1, columns] = row_max
    stat_ref[0, 1:2, columns] = row_sum


def page_counts(ids, table_ref, length, store):
    pages, lanes = ids.shape
    found = jnp.zeros((pages, lanes), jnp.int32)
    for entry in range(table_ref.shape[0]):
        left = length - entry * PAGE
        weight = jnp.where(left >= PAGE, 1, jnp.where(left > 0, CUT, 0))
        found += jnp.where(ids == table_ref[entry : entry + 1, :], weight, 0)
    whole = (found & (CUT - 1)).astype(jnp.float32)
    cut = (found // CUT).astype(jnp.float32)
    token = lax.broadcasted_iota(jnp.int32, (PAGE, lanes), 0)
    kept = (token < length % PAGE).astype(jnp.float32)
    for page in range(pages):
        one = slice(page, page + 1)
        store(page, (whole[one] + cut[one] * kept).astype(jnp.bfloat16))


def resident_kernel(
    group, query_ref, key_ref, value_ref, table_ref, length_ref, acc_ref, stat_ref, counts
):
    queries = stack_heads(query_ref, group)
    rows = queries.shape[0]
    pages = counts.shape[0] // PAGE

    @pl.when(pl.program_id(0) == 0)
    def _():
        def store(page, found):
            counts[page * PAGE : (page + 1) * PAGE] = found

        ids = lax.broadcasted_iota(jnp.int32, (pages, rows), 0)
        page_counts(ids, table_ref, length_ref[...], store)

    new_max, product = counted_piece(
        queries,
        key_ref[...],
        turned_with_ones(value_ref[...]),
        counts[...].astype(jnp.float32),
        jnp.full((1, rows), LOW, jnp.float32),
    )
    acc_ref[0] = product[:HD]
    store_stats(stat_ref, slice(0, rows), new_max, product[HD : HD + 1])


def resident_attention(decode_query, keys, values, table, lengths):
    rows, query_width = decode_query.shape
    pool_rows, key_width = keys.shape
    kv_heads = key_width // HD
    group = query_width // key_width
    entries, lanes = table.shape
    return pl.pallas_call(
        functools.partial(resident_kernel, group),
        out_shape=(
            jax.ShapeDtypeStruct((kv_heads, HD, lanes), jnp.float32),
            jax.ShapeDtypeStruct((kv_heads, 8, lanes), jnp.float32),
        ),
        grid=(kv_heads,),
        in_specs=[
            pl.BlockSpec((rows, group * HD), lambda g: (0, g)),
            pl.BlockSpec((pool_rows, HD), lambda g: (0, g)),
            pl.BlockSpec((pool_rows, HD), lambda g: (0, g)),
            pl.BlockSpec((entries, lanes), lambda g: (0, 0)),
            pl.BlockSpec((1, lanes), lambda g: (0, 0)),
        ],
        out_specs=[
            pl.BlockSpec((1, HD, lanes), lambda g: (g, 0, 0)),
            pl.BlockSpec((1, 8, lanes), lambda g: (g, 0, 0)),
        ],
        scratch_shapes=[pltpu.VMEM((pool_rows, lanes), jnp.bfloat16)],
        compiler_params=params(60 * 2**20),
        cost_estimate=pl.CostEstimate(
            flops=6 * kv_heads * lanes * pool_rows * HD,
            bytes_accessed=4 * key_width * pool_rows,
            transcendentals=kv_heads * lanes * pool_rows,
        ),
        name="resident",
    )(decode_query, keys, values, table, lengths)


def attend_kernel(n_blocks, group, tile_heads, pool, first, final, place_ref, *refs):
    refs = list(refs)

    def take(count):
        taken, refs[:count] = refs[:count], []
        return taken

    query_ref, decode_ref = take(2)
    keys = take(n_blocks)
    values = take(n_blocks)
    codes = take(n_blocks)
    table_ref, length_ref = take(2)
    if not first:
        acc_in, stat_in = take(2)
    if final:
        side_acc, side_stat = take(2)
        out_ref, decode_out = take(2)
    else:
        acc_out, stat_out = take(2)
    (counts,) = refs
    rows = query_ref.shape[0]
    decode_rows = decode_ref.shape[0]
    own = place_ref[0]

    @pl.when(pl.program_id(0) == 0)
    def _():
        for b in range(n_blocks):
            section = place_ref[1 + b]
            slot = codes[b][...].astype(jnp.float32).astype(jnp.int32) - own * CAP
            mine = (slot >= 0) & (slot < CAP)
            if not (first and b == 0):
                mine &= section != own
            ids = jnp.where(mine, pool + section * CAP + slot, -1)

            def store(page, found, b=b):
                top = b * rows + page * PAGE
                counts[top : top + PAGE] = found

            page_counts(ids, table_ref, length_ref[...], store)

    all_keys = jnp.concatenate([ref[...] for ref in keys], axis=0)
    all_values = turned_with_ones(jnp.concatenate([ref[...] for ref in values], axis=0))
    seen = [place_ref[1 + b] < own for b in range(n_blocks)]
    tile = tile_heads * rows
    for top in range(0, group * rows, tile):
        here = slice(top, top + tile)
        heads = range(top // rows, top // rows + tile_heads)
        queries = jnp.concatenate([query_ref[:, h * HD : (h + 1) * HD] for h in heads], axis=0)
        scores = lax.dot_general(all_keys, queries, NT, preferred_element_type=jnp.float32)
        span = scores.shape[0] // n_blocks
        pieces = [scores[b * span : (b + 1) * span] for b in range(n_blocks)]
        if first:
            key_of = lax.broadcasted_iota(jnp.int32, (span, rows), 0)
            row_of = lax.broadcasted_iota(jnp.int32, (span, rows), 1)
            kept = jnp.concatenate([key_of <= row_of] * tile_heads, axis=1)
            pieces[0] = jnp.where(kept, pieces[0], LOW)
            new_max = jnp.max(pieces[0], axis=0, keepdims=True) * EXP2_SCALE
        else:
            old_max = stat_in[0, 0:1, here]
            new_max = old_max
        for b in range(1 if first else 0, n_blocks):
            highest = jnp.max(pieces[b], axis=0, keepdims=True) * EXP2_SCALE
            new_max = jnp.maximum(new_max, jnp.where(seen[b], highest, LOW))
        weights = []
        for b in range(n_blocks):
            shift = new_max
            if not (first and b == 0):
                shift = new_max + jnp.where(seen[b], 0.0, -LOW)
            weights.append(jnp.exp2(pieces[b] * EXP2_SCALE - shift).astype(jnp.bfloat16))
        product = jnp.dot(
            all_values, jnp.concatenate(weights, axis=0), preferred_element_type=jnp.float32
        )
        acc, total = product[:HD], product[HD : HD + 1]
        if not first:
            fade = jnp.exp2(old_max - new_max)
            acc += acc_in[0, :, here] * fade
            total += stat_in[0, 1:2, here] * fade
        if final:
            result = (acc / total).T.astype(jnp.bfloat16)
            for place, h in enumerate(heads):
                out_ref[:, h * HD : (h + 1) * HD] = result[place * rows : (place + 1) * rows]
        else:
            acc_out[0, :, here] = acc
            store_stats(stat_out, here, new_max, total)

    queries = stack_heads(decode_ref, group)
    small = group * decode_rows
    here = slice(group * rows, group * rows + small)
    if first:
        old_max = jnp.full((1, small), LOW, jnp.float32)
    else:
        old_max = stat_in[0, 0:1, here]
    new_max, product = counted_piece(
        queries,
        all_keys,
        all_values,
        counts[...].astype(jnp.float32),
        old_max,
    )
    acc, total = product[:HD], product[HD : HD + 1]
    if not first:
        fade = jnp.exp2(old_max - new_max)
        acc += acc_in[0, :, here] * fade
        total += stat_in[0, 1:2, here] * fade
    if final:
        side_max = side_stat[0, 0:1]
        top_max = jnp.maximum(new_max, side_max)
        fade, side_fade = jnp.exp2(new_max - top_max), jnp.exp2(side_max - top_max)
        acc = acc * fade + side_acc[0] * side_fade
        total = total * fade + side_stat[0, 1:2] * side_fade
        result = (acc / total).T.astype(jnp.bfloat16)
        for h in range(group):
            decode_out[:, h * HD : (h + 1) * HD] = result[h * decode_rows : (h + 1) * decode_rows]
    else:
        acc_out[0, :, here] = acc
        store_stats(stat_out, here, new_max, total)


def attend(place, query, decode_query, blocks, table, lengths, pool, state, side, kv_heads):
    n_blocks = len(blocks)
    rows, query_width = query.shape
    decode_rows = decode_query.shape[0]
    block_rows = rows
    pages = blocks[0].shape[0] - rows
    group = query_width // (kv_heads * HD)
    first, final = state is None, side is not None
    total_rows = group * (rows + decode_rows)
    small = group * decode_rows

    def by_head(*shape):
        return pl.BlockSpec((1, *shape), lambda g, place_ref: (g, 0, 0))

    query_spec = pl.BlockSpec((rows, group * HD), lambda g, place_ref: (0, g))
    decode_spec = pl.BlockSpec((decode_rows, group * HD), lambda g, place_ref: (0, g))
    key_spec = pl.BlockSpec((block_rows, HD), lambda g, place_ref: (0, g))
    value_spec = pl.BlockSpec((block_rows, HD), lambda g, place_ref: (0, kv_heads + g))
    code_spec = pl.BlockSpec((pages, small), lambda g, place_ref: (rows // pages, 0))
    operands = [query, decode_query, *blocks, *blocks, *blocks, table, lengths]
    in_specs = [query_spec, decode_spec] + [key_spec] * n_blocks + [value_spec] * n_blocks
    in_specs += [code_spec] * n_blocks
    in_specs += [
        pl.BlockSpec(table.shape, lambda g, place_ref: (0, 0)),
        pl.BlockSpec(lengths.shape, lambda g, place_ref: (0, 0)),
    ]
    if not first:
        operands += list(state)
        in_specs += [by_head(HD, total_rows), by_head(8, total_rows)]
    if final:
        operands += list(side)
        in_specs += [by_head(HD, small), by_head(8, small)]
        out_shape = (
            jax.ShapeDtypeStruct(query.shape, jnp.bfloat16),
            jax.ShapeDtypeStruct(decode_query.shape, jnp.bfloat16),
        )
        out_specs = [query_spec, decode_spec]
    else:
        out_shape = (
            jax.ShapeDtypeStruct((kv_heads, HD, total_rows), jnp.float32),
            jax.ShapeDtypeStruct((kv_heads, 8, total_rows), jnp.float32),
        )
        out_specs = [by_head(HD, total_rows), by_head(8, total_rows)]
    tile_heads = group
    pairs = kv_heads * total_rows * n_blocks * block_rows
    return pl.pallas_call(
        functools.partial(attend_kernel, n_blocks, group, tile_heads, pool, first, final),
        out_shape=out_shape,
        grid_spec=pltpu.PrefetchScalarGridSpec(
            num_scalar_prefetch=1,
            grid=(kv_heads,),
            in_specs=in_specs,
            out_specs=out_specs,
            scratch_shapes=[pltpu.VMEM((n_blocks * rows, small), jnp.bfloat16)],
        ),
        compiler_params=params(),
        cost_estimate=pl.CostEstimate(
            flops=6 * pairs * HD,
            bytes_accessed=12 * kv_heads * total_rows * HD,
            transcendentals=pairs,
        ),
        name="attend",
    )(place, *operands)


def page_codes(page_owner):
    page_index = jnp.arange(page_owner.shape[0], dtype=jnp.int32)
    earlier = (page_owner[:, None] == page_owner[None, :]) & (
        page_index[None, :] < page_index[:, None]
    )
    return (page_owner * CAP + jnp.sum(earlier.astype(jnp.int32), axis=1)).astype(jnp.float32)


def fence(*arrays):
    return lax.optimization_barrier(arrays)


def gather_rounds(own, work):
    def settle(moved, work):
        return fence(*moved, *work)[: len(moved)]

    size_z, size_y, size_x = 4, 2, 2
    here = lax.axis_index("section")
    z, column = here // 4, here % 4

    def index(zz, yy, xx):
        return (zz * size_y + yy) * size_x + xx

    def along_z(pairs):
        return [
            (index(a, yy, xx), index(b, yy, xx))
            for a, b in pairs
            for yy in range(size_y)
            for xx in range(size_x)
        ]

    every = [(zz, yy, xx) for zz in range(size_z) for yy in range(size_y) for xx in range(size_x)]
    swap_x = [(index(zz, yy, xx), index(zz, yy, 1 - xx)) for zz, yy, xx in every]
    swap_y = [(index(zz, yy, xx), index(zz, 1 - yy, xx)) for zz, yy, xx in every]
    ends = along_z([(0, 1), (1, 0), (2, 3), (3, 2)])
    middle = along_z([(1, 2), (2, 1)])
    outward = along_z([(1, 0), (2, 3)])
    inner = (z == 1) | (z == 2)

    def move(block, pairs):
        return lax.ppermute(block, "section", pairs)

    plane_a = jnp.bitwise_xor(z, 1)
    plane_f = jnp.where(inner, 3 - z, jnp.where(z == 0, 2, 1))
    plane_g = jnp.where(inner, jnp.bitwise_xor(3 - z, 1), 3 - z)

    def at(plane, turn):
        return plane * 4 + jnp.bitwise_xor(column, turn)

    moved = move(own, swap_x), move(own, swap_y), move(own, ends), move(own, middle)
    own_x, own_y, a, b = settle(moved, work)
    work = yield [(own, here), (own_x, at(z, 1)), (own_y, at(z, 2)), (a, at(plane_a, 0))]
    moved = move(own_y, swap_x), move(a, swap_y), move(b, outward), move(a, middle)
    own_d, a_y, c, d = settle(moved, work)
    f = jnp.where(inner, b, c)
    work = yield [(own_d, at(z, 3)), (a_y, at(plane_a, 2)), (f, at(plane_f, 0))]
    either = jnp.where(inner, d, own_d)
    moved = move(a, swap_x), move(f, swap_y), move(either, ends), move(own_d, middle)
    a_x, f_y, e, b_in = settle(moved, work)
    g = jnp.where(inner, d, e)
    work = yield [(a_x, at(plane_a, 1)), (f_y, at(plane_f, 2)), (g, at(plane_g, 0))]
    moved = move(f, swap_x), move(g, swap_y), move(b_in, outward), move(e, middle)
    f_x, g_y, c_in, d_in = settle(moved, work)
    f_d = jnp.where(inner, b_in, c_in)
    work = yield [(f_x, at(plane_f, 1)), (g_y, at(plane_g, 2)), (f_d, at(plane_f, 3))]
    moved = move(g, swap_x), move(a_x, swap_y), move(d_in, outward)
    g_x, a_turn, e_in = settle(moved, work)
    a_d = jnp.where(inner, e, a_turn)
    g_d = jnp.where(inner, d_in, e_in)
    yield [(g_x, at(plane_g, 1)), (a_d, at(plane_a, 3)), (g_d, at(plane_g, 3))]


def gather_plain(own, section_count):
    rows = own.shape[0]
    gathered = lax.all_gather(own, "section", axis=0, tiled=True)
    step = math.gcd(section_count, 4)
    for top in range(0, section_count, step):
        yield [
            (gathered[s * rows : (s + 1) * rows], jnp.int32(s)) for s in range(top, top + step)
        ]


def per_device(
    prefill_hidden,
    norm_gain,
    key_weight,
    value_weight,
    prefill_query,
    resident_keys,
    resident_values,
    decode_query,
    page_owner,
    block_table,
    context_len,
):
    section_count = lax.axis_size("section")
    tp_count = lax.axis_size("tp")
    section = lax.axis_index("section").astype(jnp.int32)
    tp = lax.axis_index("tp").astype(jnp.int32)
    rows = prefill_hidden.shape[0]
    key_width = key_weight.shape[1]
    kv_heads = key_width // HD
    group = prefill_query.shape[1] // key_width
    pool = resident_keys.shape[0]

    if tp_count == 2:
        other = lax.ppermute(prefill_hidden, "tp", [(0, 1), (1, 0)])
        parts, order = [prefill_hidden, other], jnp.stack([tp, 1 - tp])
    else:
        parts = [lax.all_gather(prefill_hidden, "tp", axis=1, tiled=True)]
        order = jnp.zeros((1,), jnp.int32)
    half = HD // 2
    frequency = jnp.exp(jnp.arange(half, dtype=jnp.float32) * (-2.0 * math.log(ROPE_THETA) / HD))
    positions = section * rows + jnp.arange(rows, dtype=jnp.int32)
    angles = positions.astype(jnp.float32)[:, None] * frequency[None, :]
    cosine, sine = jnp.cos(angles), jnp.sin(angles)
    cosine = jnp.concatenate([cosine, cosine], axis=1)
    sine = jnp.concatenate([-sine, sine], axis=1)

    key_near, value_near = stage(key_weight, value_weight)
    own = project(
        parts,
        order,
        norm_gain,
        key_near,
        value_near,
        cosine,
        sine,
        page_codes(page_owner).reshape(-1, 1),
    )

    own, block_table, context_len = fence(own, block_table, context_len)
    table = jnp.concatenate([block_table] * group, axis=0).T
    lengths = jnp.concatenate([context_len] * group)[None, :]
    side = resident_attention(
        decode_query,
        resident_keys.reshape(pool * PAGE, key_width),
        resident_values.reshape(pool * PAGE, key_width),
        table,
        lengths,
    )

    def step(arrived, state, side):
        place = jnp.stack([section] + [s.astype(jnp.int32) for _, s in arrived])
        blocks = [block for block, _ in arrived]
        return attend(
            place, prefill_query, decode_query, blocks, table, lengths, pool, state, side, kv_heads
        )

    if section_count == 16:
        rounds = gather_rounds(own, side)
        arrived, state = next(rounds), None
        for _ in range(4):
            state = step(arrived, state, None)
            arrived = rounds.send(state)
        return step(arrived, state, side)
    state = step([(own, section)], None, None)
    rounds = list(gather_plain(own, section_count))
    for arrived in rounds[:-1]:
        state = step(arrived, state, None)
    return step(rounds[-1], state, side)


def solution(mesh):
    return jax.shard_map(
        per_device,
        mesh=mesh,
        in_specs=(
            P("section", "tp"),
            P(),
            P(None, "tp"),
            P(None, "tp"),
            P("section", "tp"),
            P("section", None, "tp"),
            P("section", None, "tp"),
            P("section", "tp"),
            P("section"),
            P("section", None),
            P("section"),
        ),
        out_specs=(P("section", "tp"), P("section", "tp")),
        check_vma=False,
    )
```

```python
import functools
import math

import jax
import jax.numpy as jnp
from jax import lax
from jax.experimental import pallas as pl
from jax.experimental.pallas import tpu as pltpu
from jax.sharding import PartitionSpec as P

HD = 128
PAGE = 16
CAP = 2
CUT = 1024
NORM_EPSILON = 1e-05
ROPE_THETA = 500000.0
LOW = -1e30
EXP2_SCALE = math.log2(math.e) / math.sqrt(HD)
VMEM_BYTES = 32 * 1024 * 1024
NT = (((1,), (1,)), ((), ()))


def params(limit=VMEM_BYTES):
    return pltpu.CompilerParams(vmem_limit_bytes=limit)


def stage_kernel(n_arrays, *refs):
    copies = [
        pltpu.make_async_copy(refs[i], refs[n_arrays + i], refs[2 * n_arrays].at[i])
        for i in range(n_arrays)
    ]
    for copy in copies:
        copy.start()
    for copy in copies:
        copy.wait()


def stage(*arrays):
    return pl.pallas_call(
        functools.partial(stage_kernel, len(arrays)),
        out_shape=tuple(jax.ShapeDtypeStruct(a.shape, a.dtype) for a in arrays),
        in_specs=[pl.BlockSpec(memory_space=pl.ANY)] * len(arrays),
        out_specs=[pl.BlockSpec(memory_space=pltpu.VMEM)] * len(arrays),
        scratch_shapes=[pltpu.SemaphoreType.DMA((len(arrays),))],
        compiler_params=params(),
        cost_estimate=pl.CostEstimate(
            flops=0, bytes_accessed=sum(2 * a.size * a.dtype.itemsize for a in arrays), transcendentals=0
        ),
        name="stage",
    )(*arrays)


def project_kernel(n_parts, chunk, order_ref, *refs):
    parts = refs[:n_parts]
    gain_ref, key_ref, value_ref, cos_ref, sin_ref, column_ref, row_ref = refs[n_parts:-2]
    out_ref, total_ref = refs[-2:]
    rows, part_width = parts[0].shape
    key_width = key_ref.shape[1]
    pages = column_ref.shape[0]
    earlier = lax.broadcasted_iota(jnp.int32, (pages, pages), 1) < lax.broadcasted_iota(
        jnp.int32, (pages, pages), 0
    )
    same = earlier & (column_ref[...] == row_ref[...])
    rank = jnp.sum(same.astype(jnp.float32), axis=1, keepdims=True)
    codes = column_ref[...].astype(jnp.float32) * CAP + rank
    out_ref[rows:] = jnp.broadcast_to(codes, (pages, 2 * key_width)).astype(jnp.bfloat16)
    squares = jnp.zeros((rows, HD), jnp.float32)
    for part in parts:
        for first in range(0, part_width, HD):
            piece = part[:, first : first + HD].astype(jnp.float32)
            squares += piece * piece
    squares = jnp.sum(squares, axis=1, keepdims=True)
    inverse = lax.rsqrt(squares * (1.0 / (part_width * n_parts)) + NORM_EPSILON)
    for index, part in enumerate(parts):
        base = order_ref[index] * part_width
        for first in range(0, part_width, chunk):
            where = pl.multiple_of(base + first, chunk)
            piece = part[:, first : first + chunk].astype(jnp.float32)
            normed = (piece * inverse * gain_ref[:, pl.ds(where, chunk)]).astype(jnp.bfloat16)
            keys = jnp.dot(
                normed, key_ref[pl.ds(where, chunk)], preferred_element_type=jnp.float32
            )
            values = jnp.dot(
                normed, value_ref[pl.ds(where, chunk)], preferred_element_type=jnp.float32
            )
            if index == 0 and first == 0:
                total_ref[:, :key_width] = keys
                total_ref[:, key_width:] = values
            else:
                total_ref[:, :key_width] += keys
                total_ref[:, key_width:] += values
    for head in range(key_width // HD):
        cut = slice(head * HD, (head + 1) * HD)
        raw = total_ref[:, cut]
        turned = raw * cos_ref[...] + pltpu.roll(raw, HD // 2, 1) * sin_ref[...]
        out_ref[:rows, cut] = turned.astype(jnp.bfloat16)
    out_ref[:rows, key_width:] = total_ref[:, key_width:].astype(jnp.bfloat16)


def project(parts, order, norm_gain, key_weight, value_weight, cosine, sine, page_owner):
    rows, part_width = parts[0].shape
    n_parts = len(parts)
    key_width = key_weight.shape[1]
    vmem = pl.BlockSpec(memory_space=pltpu.VMEM)
    pages = page_owner.shape[0]
    return pl.pallas_call(
        functools.partial(project_kernel, n_parts, math.gcd(part_width, 1024)),
        out_shape=jax.ShapeDtypeStruct((rows + pages, 2 * key_width), jnp.bfloat16),
        in_specs=[pl.BlockSpec(memory_space=pltpu.SMEM)] + [vmem] * (n_parts + 7),
        out_specs=vmem,
        scratch_shapes=[pltpu.VMEM((rows, 2 * key_width), jnp.float32)],
        compiler_params=params(),
        cost_estimate=pl.CostEstimate(
            flops=4 * rows * key_width * part_width * n_parts,
            bytes_accessed=4 * key_width * part_width * n_parts,
            transcendentals=0,
        ),
        name="project",
    )(
        order,
        *parts,
        norm_gain.reshape(1, -1),
        key_weight,
        value_weight,
        cosine,
        sine,
        page_owner.reshape(-1, 1),
        page_owner.reshape(1, -1),
    )


def stack_heads(ref, group):
    return jnp.concatenate([ref[:, h * HD : (h + 1) * HD] for h in range(group)], axis=0)


def turned_with_ones(values):
    turned = values.T
    return jnp.concatenate([turned, jnp.ones((16, turned.shape[1]), turned.dtype)], axis=0)


def counted_piece(queries, keys, values_ones, bias, old_max):
    scores = lax.dot_general(keys, queries, NT, preferred_element_type=jnp.float32)
    scores = scores * EXP2_SCALE + bias
    new_max = jnp.maximum(old_max, jnp.max(scores, axis=0, keepdims=True))
    weights = jnp.exp2(scores - new_max).astype(jnp.bfloat16)
    product = jnp.dot(values_ones, weights, preferred_element_type=jnp.float32)
    return new_max, product


def store_stats(stat_ref, columns, row_max, row_sum):
    stat_ref[0, 0:1, columns] = row_max
    stat_ref[0, 1:2, columns] = row_sum


def page_bias(ids, table_ref, length, store):
    pages, lanes = ids.shape
    found = jnp.zeros((pages, lanes), jnp.int32)
    for entry in range(table_ref.shape[0]):
        left = length - entry * PAGE
        weight = jnp.where(left >= PAGE, 1, jnp.where(left > 0, CUT, 0))
        found += jnp.where(ids == table_ref[entry : entry + 1, :], weight, 0)

    def logarithm(count):
        return jnp.where(count > 0, jnp.log2(jnp.maximum(count, 1).astype(jnp.float32)), LOW)

    whole = found & (CUT - 1)
    with_cut = logarithm(whole + lax.shift_right_logical(found, CUT.bit_length() - 1))
    whole = logarithm(whole)
    token = lax.broadcasted_iota(jnp.int32, (PAGE, lanes), 0)
    kept = token < length % PAGE
    for page in range(pages):
        one = slice(page, page + 1)
        store(page, jnp.where(kept, with_cut[one], whole[one]))


def resident_kernel(
    group, pool, slot_ref, query_ref, key_ref, value_ref, table_ref, length_ref, *refs
):
    acc_ref, stat_ref, slot_bias_ref, bias = refs
    step = pl.program_id(0)
    pages, lanes = bias.shape[0] // PAGE, bias.shape[1]

    @pl.when(step == 0)
    def _():
        acc_ref[...] = jnp.zeros_like(acc_ref)
        stat_ref[:, 0:1] = jnp.full_like(stat_ref[:, 0:1], LOW)
        stat_ref[:, 1:2] = jnp.zeros_like(stat_ref[:, 1:2])
        slots = slot_bias_ref.shape[0] // PAGE
        slot_of = lax.broadcasted_iota(jnp.int32, (slots, lanes), 0)
        ids = slot_of % CAP
        for block in range(slots // CAP):
            ids += jnp.where(slot_of // CAP == block, pool + slot_ref[block] * CAP, 0)

        def store_slot(page, found):
            slot_bias_ref[page * PAGE : (page + 1) * PAGE] = found

        page_bias(ids, table_ref, length_ref[...], store_slot)

    def store(page, found):
        bias[page * PAGE : (page + 1) * PAGE] = found

    ids = step * pages + lax.broadcasted_iota(jnp.int32, (pages, lanes), 0)
    page_bias(ids, table_ref, length_ref[...], store)
    for head in range(key_ref.shape[1] // HD):
        cut = slice(head * HD, (head + 1) * HD)
        queries = jnp.concatenate(
            [
                query_ref[:, (head * group + h) * HD : (head * group + h + 1) * HD]
                for h in range(group)
            ],
            axis=0,
        )
        old_max = stat_ref[head, 0:1]
        new_max, product = counted_piece(
            queries, key_ref[:, cut], turned_with_ones(value_ref[:, cut]), bias[...], old_max
        )
        fade = jnp.exp2(old_max - new_max)
        acc_ref[head] = acc_ref[head] * fade + product[:HD]
        stat_ref[head, 1:2] = stat_ref[head, 1:2] * fade + product[HD : HD + 1]
        stat_ref[head, 0:1] = new_max


def resident_attention(decode_query, keys, values, table, lengths, slots, pool):
    pool_rows, key_width = keys.shape
    kv_heads = key_width // HD
    group = decode_query.shape[1] // key_width
    lanes = table.shape[1]
    steps = math.gcd(pool, 4)
    chunk = pool_rows // steps

    def whole(*shape):
        return pl.BlockSpec(shape, lambda step, _: (0,) * len(shape))

    piece = pl.BlockSpec((chunk, key_width), lambda step, _: (step, 0))
    shapes = [(kv_heads, HD, lanes), (kv_heads, 8, lanes), (slots.shape[0] * CAP * PAGE, lanes)]
    return pl.pallas_call(
        functools.partial(resident_kernel, group, pool),
        out_shape=tuple(jax.ShapeDtypeStruct(shape, jnp.float32) for shape in shapes),
        grid_spec=pltpu.PrefetchScalarGridSpec(
            num_scalar_prefetch=1,
            grid=(steps,),
            in_specs=[whole(*decode_query.shape), piece, piece]
            + [whole(*table.shape), whole(*lengths.shape)],
            out_specs=[whole(*shape) for shape in shapes],
            scratch_shapes=[pltpu.VMEM((chunk, lanes), jnp.float32)],
        ),
        compiler_params=params(60 * 2**20),
        cost_estimate=pl.CostEstimate(
            flops=6 * kv_heads * lanes * pool_rows * HD,
            bytes_accessed=4 * key_width * pool_rows,
            transcendentals=kv_heads * lanes * pool_rows,
        ),
        name="resident",
    )(slots, decode_query, keys, values, table, lengths)


def pages_here(code_ref, key_ref, value_ref, own, rows):
    codes = code_ref[...].astype(jnp.float32).astype(jnp.int32)
    found = []
    for slot in range(CAP):
        mine = codes == own * CAP + slot
        both = [jnp.zeros((PAGE, HD), jnp.float32)] * 2
        for page in range(rows // PAGE):
            here = jnp.broadcast_to(mine[page : page + 1], (PAGE, HD))
            cut = slice(page * PAGE, (page + 1) * PAGE)
            both = [
                jnp.where(here, ref[cut].astype(jnp.float32), held)
                for ref, held in zip((key_ref, value_ref), both)
            ]
        found.append(jnp.concatenate(both, axis=1))
    return jnp.concatenate(found, axis=0).astype(jnp.bfloat16)


def attend_kernel(n_blocks, n_pages, group, first, final, place_ref, *refs):
    refs = list(refs)

    def take(count):
        taken, refs[:count] = refs[:count], []
        return taken

    (query_ref,) = take(1)
    keys = take(n_blocks)
    values = take(n_blocks)
    codes = take(n_blocks)
    if not first:
        acc_in, stat_in = take(2)
    if final:
        decode_ref, side_acc, side_stat, bias_ref = take(4)
        pages = take(n_pages)
        out_ref, decode_out = refs
    else:
        acc_out, stat_out, page_out = refs
    rows = query_ref.shape[0]
    own = place_ref[0]
    all_keys = jnp.concatenate([ref[...] for ref in keys], axis=0)
    all_values = turned_with_ones(jnp.concatenate([ref[...] for ref in values], axis=0))
    seen = [place_ref[1 + b] < own for b in range(n_blocks)]
    span = rows
    queries = stack_heads(query_ref, group)
    scores = lax.dot_general(all_keys, queries, NT, preferred_element_type=jnp.float32)
    pieces = [scores[b * span : (b + 1) * span] for b in range(n_blocks)]
    if first:
        key_of = lax.broadcasted_iota(jnp.int32, (span, rows), 0)
        row_of = lax.broadcasted_iota(jnp.int32, (span, rows), 1)
        kept = jnp.concatenate([key_of <= row_of] * group, axis=1)
        pieces[0] = jnp.where(kept, pieces[0], LOW)
        new_max = jnp.max(pieces[0], axis=0, keepdims=True) * EXP2_SCALE
    else:
        old_max = stat_in[0, 0:1]
        new_max = old_max
    for b in range(1 if first else 0, n_blocks):
        highest = jnp.max(pieces[b], axis=0, keepdims=True) * EXP2_SCALE
        new_max = jnp.maximum(new_max, jnp.where(seen[b], highest, LOW))
    weights = []
    for b in range(n_blocks):
        shift = new_max
        if not (first and b == 0):
            shift = new_max + jnp.where(seen[b], 0.0, -LOW)
        weights.append(jnp.exp2(pieces[b] * EXP2_SCALE - shift).astype(jnp.bfloat16))
    product = jnp.dot(
        all_values, jnp.concatenate(weights, axis=0), preferred_element_type=jnp.float32
    )
    acc, total = product[:HD], product[HD : HD + 1]
    if not first:
        fade = jnp.exp2(old_max - new_max)
        acc += acc_in[0] * fade
        total += stat_in[0, 1:2] * fade
    new_pages = jnp.concatenate(
        [pages_here(codes[b], keys[b], values[b], own, rows) for b in range(n_blocks)], axis=0
    )
    if not final:
        acc_out[0] = acc
        store_stats(stat_out, slice(None), new_max, total)
        page_out[0] = new_pages
        return

    result = (acc * (1.0 / total)).astype(jnp.bfloat16)
    for h in range(group):
        out_ref[:, h * HD : (h + 1) * HD] = (
            result[:, h * rows : (h + 1) * rows].T
        )

    decode_rows = decode_ref.shape[0]

    all_pages = jnp.concatenate([ref[0] for ref in pages] + [new_pages], axis=0)
    queries = stack_heads(decode_ref, group)
    side_max = side_stat[0, 0:1]
    new_max, product = counted_piece(
        queries,
        all_pages[:, :HD],
        turned_with_ones(all_pages[:, HD:]),
        bias_ref[...],
        side_max,
    )
    fade = jnp.exp2(side_max - new_max)
    acc = product[:HD] + side_acc[0] * fade
    total = product[HD : HD + 1] + side_stat[0, 1:2] * fade
    result = (acc / total).T.astype(jnp.bfloat16)
    for h in range(group):
        decode_out[:, h * HD : (h + 1) * HD] = result[h * decode_rows : (h + 1) * decode_rows]


def attend(arrived, section, query, state, decode, kv_heads):
    blocks = [block for block, _ in arrived]
    place = jnp.stack([section] + [s.astype(jnp.int32) for _, s in arrived])
    n_blocks = len(blocks)
    rows, query_width = query.shape
    group = query_width // (kv_heads * HD)
    pages = blocks[0].shape[0] - rows
    first, final = state is None, decode is not None
    total_rows = group * rows
    page_rows = n_blocks * CAP * PAGE

    def by_head(*shape):
        return pl.BlockSpec((1, *shape), lambda g, *_: (g, 0, 0))

    def whole(array):
        return pl.BlockSpec(array.shape, lambda g, *_: (0, 0))

    query_spec = pl.BlockSpec((rows, group * HD), lambda g, *_: (0, g))
    key_spec = pl.BlockSpec((rows, HD), lambda g, *_: (0, g))
    value_spec = pl.BlockSpec((rows, HD), lambda g, *_: (0, kv_heads + g))
    code_spec = pl.BlockSpec((pages, HD), lambda g, *_: (rows // pages, 0))
    operands = [query, *blocks, *blocks, *blocks]
    in_specs = [query_spec] + [key_spec] * n_blocks + [value_spec] * n_blocks
    in_specs += [code_spec] * n_blocks
    held = []
    if not first:
        acc, stats, held = state
        operands += [acc, stats]
        in_specs += [by_head(HD, total_rows), by_head(8, total_rows)]
    if final:
        decode_query, side_acc, side_stat, bias = decode
        small = bias.shape[1]
        decode_spec = pl.BlockSpec((decode_query.shape[0], group * HD), lambda g, *_: (0, g))
        operands += [decode_query, side_acc, side_stat, bias, *held]
        in_specs += [decode_spec, by_head(HD, small), by_head(8, small), whole(bias)]
        in_specs += [by_head(*array.shape[1:]) for array in held]
        out_shape = (
            jax.ShapeDtypeStruct(query.shape, jnp.bfloat16),
            jax.ShapeDtypeStruct(decode_query.shape, jnp.bfloat16),
        )
        out_specs = [query_spec, decode_spec]
    else:
        out_shape = (
            jax.ShapeDtypeStruct((kv_heads, HD, total_rows), jnp.float32),
            jax.ShapeDtypeStruct((kv_heads, 8, total_rows), jnp.float32),
            jax.ShapeDtypeStruct((kv_heads, page_rows, 2 * HD), jnp.bfloat16),
        )
        out_specs = [by_head(*shape.shape[1:]) for shape in out_shape]
    pairs = kv_heads * total_rows * n_blocks * rows
    result = pl.pallas_call(
        functools.partial(attend_kernel, n_blocks, len(held), group, first, final),
        out_shape=out_shape,
        grid_spec=pltpu.PrefetchScalarGridSpec(
            num_scalar_prefetch=1,
            grid=(kv_heads,),
            in_specs=in_specs,
            out_specs=out_specs,
        ),
        compiler_params=params(),
        cost_estimate=pl.CostEstimate(
            flops=6 * pairs * HD,
            bytes_accessed=12 * kv_heads * total_rows * HD,
            transcendentals=pairs,
        ),
        name="attend",
    )(place, *operands)
    if final:
        return result
    return result[0], result[1], [*held, result[2]]


def fence(*arrays):
    return lax.optimization_barrier(arrays)


def grid_sections():
    here = lax.axis_index("section")
    z, column = here // 4, here % 4
    inner = (z == 1) | (z == 2)
    plane_a = jnp.bitwise_xor(z, 1)
    plane_f = jnp.where(inner, 3 - z, jnp.where(z == 0, 2, 1))
    plane_g = jnp.where(inner, jnp.bitwise_xor(3 - z, 1), 3 - z)
    order = [(z, 0), (z, 1), (z, 2), (plane_a, 0), (z, 3), (plane_a, 2), (plane_f, 0)]
    order += [(plane_a, 1), (plane_f, 2), (plane_g, 0), (plane_f, 1), (plane_g, 2), (plane_f, 3)]
    order += [(plane_g, 1), (plane_a, 3), (plane_g, 3)]
    return [plane * 4 + jnp.bitwise_xor(column, turn) for plane, turn in order]


def gather_rounds(own, sections, work):
    sections = iter(sections)

    def named(*blocks):
        return [(block, next(sections)) for block in blocks]

    def settle(moved, work, *kept):
        return fence(*moved, *kept, *work)[: len(moved) + len(kept)]

    size_z, size_y, size_x = 4, 2, 2
    z = lax.axis_index("section") // 4

    def index(zz, yy, xx):
        return (zz * size_y + yy) * size_x + xx

    def along_z(pairs):
        return [
            (index(a, yy, xx), index(b, yy, xx))
            for a, b in pairs
            for yy in range(size_y)
            for xx in range(size_x)
        ]

    every = [(zz, yy, xx) for zz in range(size_z) for yy in range(size_y) for xx in range(size_x)]
    swap_x = [(index(zz, yy, xx), index(zz, yy, 1 - xx)) for zz, yy, xx in every]
    swap_y = [(index(zz, yy, xx), index(zz, 1 - yy, xx)) for zz, yy, xx in every]
    ends = along_z([(0, 1), (1, 0), (2, 3), (3, 2)])
    middle = along_z([(1, 2), (2, 1)])
    outward = along_z([(1, 0), (2, 3)])
    inner = (z == 1) | (z == 2)

    def move(block, pairs):
        return lax.ppermute(block, "section", pairs)

    moved = move(own, swap_x), move(own, swap_y), move(own, ends), move(own, middle)
    own_x, own_y, a, b = settle(moved, work)
    work = yield named(own, own_x, own_y, a)
    moved = move(own_y, swap_x), move(a, swap_y), move(b, outward), move(a, middle)
    own_d, a_y, c, d, a, b = settle(moved, work, a, b)
    f = jnp.where(inner, b, c)
    work = yield named(own_d, a_y, f)
    either = jnp.where(inner, d, own_d)
    moved = move(a, swap_x), move(f, swap_y), move(either, ends), move(own_d, middle)
    a_x, f_y, e, b_in, f, d = settle(moved, work, f, d)
    g = jnp.where(inner, d, e)
    work = yield named(a_x, f_y, g)
    moved = move(f, swap_x), move(g, swap_y), move(b_in, outward), move(e, middle)
    f_x, g_y, c_in, d_in, g, a_x, b_in, e = settle(moved, work, g, a_x, b_in, e)
    f_d = jnp.where(inner, b_in, c_in)
    work = yield named(f_x, g_y, f_d)
    moved = move(g, swap_x), move(a_x, swap_y), move(d_in, outward)
    g_x, a_turn, e_in = settle(moved, work)
    a_d = jnp.where(inner, e, a_turn)
    g_d = jnp.where(inner, d_in, e_in)
    yield named(g_x, a_d, g_d)


def plain_sections(section_count, section, pool):
    every = [jnp.int32(s) for s in range(section_count)]
    return [jnp.where(s == section, -pool, s) for s in every]


def gather_plain(own, section_count):
    rows = own.shape[0]
    gathered = lax.all_gather(own, "section", axis=0, tiled=True)
    step = math.gcd(section_count, 4)
    for top in range(0, section_count, step):
        yield [
            (gathered[s * rows : (s + 1) * rows], jnp.int32(s)) for s in range(top, top + step)
        ]


def per_device(
    prefill_hidden,
    norm_gain,
    key_weight,
    value_weight,
    prefill_query,
    resident_keys,
    resident_values,
    decode_query,
    page_owner,
    block_table,
    context_len,
):
    section_count = lax.axis_size("section")
    tp_count = lax.axis_size("tp")
    section = lax.axis_index("section").astype(jnp.int32)
    tp = lax.axis_index("tp").astype(jnp.int32)
    rows = prefill_hidden.shape[0]
    key_width = key_weight.shape[1]
    kv_heads = key_width // HD
    group = prefill_query.shape[1] // key_width
    pool = resident_keys.shape[0]

    if tp_count == 2:
        other = lax.ppermute(prefill_hidden, "tp", [(0, 1), (1, 0)])
        parts, order = [prefill_hidden, other], jnp.stack([tp, 1 - tp])
    else:
        parts = [lax.all_gather(prefill_hidden, "tp", axis=1, tiled=True)]
        order = jnp.zeros((1,), jnp.int32)
    half = HD // 2
    frequency = jnp.exp(jnp.arange(half, dtype=jnp.float32) * (-2.0 * math.log(ROPE_THETA) / HD))
    positions = section * rows + jnp.arange(rows, dtype=jnp.int32)
    angles = positions.astype(jnp.float32)[:, None] * frequency[None, :]
    cosine, sine = jnp.cos(angles), jnp.sin(angles)
    cosine = jnp.concatenate([cosine, cosine], axis=1)
    sine = jnp.concatenate([-sine, sine], axis=1)

    key_near, value_near = stage(key_weight, value_weight)
    own = project(
        parts, order, norm_gain, key_near, value_near, cosine, sine, page_owner
    )

    own, block_table, context_len = fence(own, block_table, context_len)
    table = jnp.concatenate([block_table] * group, axis=0).T
    lengths = jnp.concatenate([context_len] * group)[None, :]
    if section_count == 16:
        sections = grid_sections()
    else:
        sections = [section] + plain_sections(section_count, section, pool)
    decode = (
        decode_query,
        *resident_attention(
            decode_query,
            resident_keys.reshape(pool * PAGE, key_width),
            resident_values.reshape(pool * PAGE, key_width),
            table,
            lengths,
            jnp.stack(sections).astype(jnp.int32),
            pool,
        ),
    )

    def step(arrived, state, last=False):
        return attend(arrived, section, prefill_query, state, decode if last else None, kv_heads)

    if section_count == 16:
        rounds = gather_rounds(own, sections, decode[1:])
        arrived, state = next(rounds), None
        for _ in range(4):
            state = step(arrived, state)
            arrived = rounds.send((state[0], state[1]))
        return step(arrived, state, True)
    state = step([(own, section)], None)
    rounds = list(gather_plain(own, section_count))
    for arrived in rounds[:-1]:
        state = step(arrived, state)
    return step(rounds[-1], state, True)


def solution(mesh):
    return jax.shard_map(
        per_device,
        mesh=mesh,
        in_specs=(
            P("section", "tp"),
            P(),
            P(None, "tp"),
            P(None, "tp"),
            P("section", "tp"),
            P("section", None, "tp"),
            P("section", None, "tp"),
            P("section", "tp"),
            P("section"),
            P("section", None),
            P("section"),
        ),
        out_specs=(P("section", "tp"), P("section", "tp")),
        check_vma=False,
    )
```

```python
import functools
import math

import jax
import jax.numpy as jnp
from jax import lax
from jax.experimental import pallas as pl
from jax.experimental.pallas import tpu as pltpu
from jax.sharding import PartitionSpec as P

HD = 128
PAGE = 16
CAP = 2
CUT = 1024
NORM_EPSILON = 1e-05
ROPE_THETA = 500000.0
LOW = -1e30
EXP2_SCALE = math.log2(math.e) / math.sqrt(HD)
VMEM_BYTES = 32 * 1024 * 1024
NT = (((1,), (1,)), ((), ()))


def params(limit=VMEM_BYTES):
    return pltpu.CompilerParams(vmem_limit_bytes=limit)


def stage_kernel(n_arrays, *refs):
    copies = [
        pltpu.make_async_copy(refs[i], refs[n_arrays + i], refs[2 * n_arrays].at[i])
        for i in range(n_arrays)
    ]
    for copy in copies:
        copy.start()
    for copy in copies:
        copy.wait()


def stage(*arrays):
    return pl.pallas_call(
        functools.partial(stage_kernel, len(arrays)),
        out_shape=tuple(jax.ShapeDtypeStruct(a.shape, a.dtype) for a in arrays),
        in_specs=[pl.BlockSpec(memory_space=pl.ANY)] * len(arrays),
        out_specs=[pl.BlockSpec(memory_space=pltpu.VMEM)] * len(arrays),
        scratch_shapes=[pltpu.SemaphoreType.DMA((len(arrays),))],
        compiler_params=params(),
        cost_estimate=pl.CostEstimate(
            flops=0, bytes_accessed=sum(2 * a.size * a.dtype.itemsize for a in arrays), transcendentals=0
        ),
        name="stage",
    )(*arrays)


def project_kernel(n_parts, chunk, order_ref, *refs):
    parts = refs[:n_parts]
    gain_ref, key_ref, value_ref, cos_ref, sin_ref, column_ref, row_ref = refs[n_parts:-2]
    out_ref, total_ref = refs[-2:]
    rows, part_width = parts[0].shape
    key_width = key_ref.shape[1]
    pages = column_ref.shape[0]
    earlier = lax.broadcasted_iota(jnp.int32, (pages, pages), 1) < lax.broadcasted_iota(
        jnp.int32, (pages, pages), 0
    )
    same = earlier & (column_ref[...] == row_ref[...])
    rank = jnp.sum(same.astype(jnp.float32), axis=1, keepdims=True)
    codes = column_ref[...].astype(jnp.float32) * CAP + rank
    out_ref[rows:] = jnp.broadcast_to(codes, (pages, 2 * key_width)).astype(jnp.bfloat16)
    squares = jnp.zeros((rows, HD), jnp.float32)
    for part in parts:
        for first in range(0, part_width, HD):
            piece = part[:, first : first + HD].astype(jnp.float32)
            squares += piece * piece
    squares = jnp.sum(squares, axis=1, keepdims=True)
    inverse = lax.rsqrt(squares * (1.0 / (part_width * n_parts)) + NORM_EPSILON)
    for index, part in enumerate(parts):
        base = order_ref[index] * part_width
        for first in range(0, part_width, chunk):
            where = pl.multiple_of(base + first, chunk)
            piece = part[:, first : first + chunk].astype(jnp.float32)
            normed = (piece * inverse * gain_ref[:, pl.ds(where, chunk)]).astype(jnp.bfloat16)
            keys = jnp.dot(
                normed, key_ref[pl.ds(where, chunk)], preferred_element_type=jnp.float32
            )
            values = jnp.dot(
                normed, value_ref[pl.ds(where, chunk)], preferred_element_type=jnp.float32
            )
            if index == 0 and first == 0:
                total_ref[:, :key_width] = keys
                total_ref[:, key_width:] = values
            else:
                total_ref[:, :key_width] += keys
                total_ref[:, key_width:] += values
    for head in range(key_width // HD):
        cut = slice(head * HD, (head + 1) * HD)
        raw = total_ref[:, cut]
        turned = raw * cos_ref[...] + pltpu.roll(raw, HD // 2, 1) * sin_ref[...]
        out_ref[:rows, cut] = turned.astype(jnp.bfloat16)
    out_ref[:rows, key_width:] = total_ref[:, key_width:].astype(jnp.bfloat16)


def project(parts, order, norm_gain, key_weight, value_weight, cosine, sine, page_owner):
    rows, part_width = parts[0].shape
    n_parts = len(parts)
    key_width = key_weight.shape[1]
    vmem = pl.BlockSpec(memory_space=pltpu.VMEM)
    pages = page_owner.shape[0]
    return pl.pallas_call(
        functools.partial(project_kernel, n_parts, math.gcd(part_width, 1024)),
        out_shape=jax.ShapeDtypeStruct((rows + pages, 2 * key_width), jnp.bfloat16),
        in_specs=[pl.BlockSpec(memory_space=pltpu.SMEM)] + [vmem] * (n_parts + 7),
        out_specs=vmem,
        scratch_shapes=[pltpu.VMEM((rows, 2 * key_width), jnp.float32)],
        compiler_params=params(),
        cost_estimate=pl.CostEstimate(
            flops=4 * rows * key_width * part_width * n_parts,
            bytes_accessed=4 * key_width * part_width * n_parts,
            transcendentals=0,
        ),
        name="project",
    )(
        order,
        *parts,
        norm_gain.reshape(1, -1),
        key_weight,
        value_weight,
        cosine,
        sine,
        page_owner.reshape(-1, 1),
        page_owner.reshape(1, -1),
    )


def turned_with_ones(values):
    turned = values.T
    return jnp.concatenate([turned, jnp.ones((16, turned.shape[1]), turned.dtype)], axis=0)


def counted_piece(queries, keys, values_ones, factor, bias, old_max):
    scores = lax.dot_general(keys, queries, NT, preferred_element_type=jnp.float32)
    scores = scores * factor + bias
    new_max = jnp.maximum(old_max, jnp.max(scores, axis=0, keepdims=True))
    weights = jnp.exp2(scores - new_max).astype(jnp.bfloat16)
    product = jnp.dot(values_ones, weights, preferred_element_type=jnp.float32)
    return new_max, product


def page_bias(ids, table_ref, length, store):
    pages, lanes = ids.shape
    found = jnp.zeros((pages, lanes), jnp.int32)
    for entry in range(table_ref.shape[0]):
        left = length - entry * PAGE
        weight = jnp.where(left >= PAGE, 1, jnp.where(left > 0, CUT, 0))
        found += jnp.where(ids == table_ref[entry : entry + 1, :], weight, 0)

    def logarithm(count):
        return jnp.where(count > 0, jnp.log2(jnp.maximum(count, 1).astype(jnp.float32)), LOW)

    whole = found & (CUT - 1)
    with_cut = logarithm(whole + lax.shift_right_logical(found, CUT.bit_length() - 1))
    whole = logarithm(whole)
    token = lax.broadcasted_iota(jnp.int32, (PAGE, lanes), 0)
    kept = token < length % PAGE
    for page in range(pages):
        one = slice(page, page + 1)
        store(page, jnp.where(kept, with_cut[one], whole[one]))


def resident_kernel(
    group, pool, slot_ref, query_ref, key_ref, value_ref, table_ref, length_ref, *refs
):
    acc_ref, stat_ref, slot_bias_ref, bias = refs
    step = pl.program_id(0)
    pages, lanes = bias.shape[0] // PAGE, bias.shape[1]

    @pl.when(step == 0)
    def _():
        acc_ref[...] = jnp.zeros_like(acc_ref)
        stat_ref[:, 0:1] = jnp.full_like(stat_ref[:, 0:1], LOW)
        stat_ref[:, 1:2] = jnp.zeros_like(stat_ref[:, 1:2])
        slots = slot_bias_ref.shape[0] // PAGE
        slot_of = lax.broadcasted_iota(jnp.int32, (slots, lanes), 0)
        ids = slot_of % CAP
        for block in range(slots // CAP):
            ids += jnp.where(slot_of // CAP == block, pool + slot_ref[block] * CAP, 0)

        def store_slot(page, found):
            slot_bias_ref[page * PAGE : (page + 1) * PAGE] = found

        page_bias(ids, table_ref, length_ref[...], store_slot)

    def store(page, found):
        bias[page * PAGE : (page + 1) * PAGE] = found

    ids = step * pages + lax.broadcasted_iota(jnp.int32, (pages, lanes), 0)
    page_bias(ids, table_ref, length_ref[...], store)
    for head in range(key_ref.shape[1] // HD):
        cut = slice(head * HD, (head + 1) * HD)
        queries = jnp.concatenate(
            [
                query_ref[:, (head * group + h) * HD : (head * group + h + 1) * HD]
                for h in range(group)
            ],
            axis=0,
        )
        old_max = stat_ref[head, 0:1]
        new_max, product = counted_piece(
            queries,
            key_ref[:, cut],
            turned_with_ones(value_ref[:, cut]),
            EXP2_SCALE,
            bias[...],
            old_max,
        )
        fade = jnp.exp2(old_max - new_max)
        acc_ref[head] = acc_ref[head] * fade + product[:HD]
        stat_ref[head, 1:2] = stat_ref[head, 1:2] * fade + product[HD : HD + 1]
        stat_ref[head, 0:1] = new_max


def resident_attention(decode_query, keys, values, table, lengths, slots, pool):
    pool_rows, key_width = keys.shape
    kv_heads = key_width // HD
    group = decode_query.shape[1] // key_width
    lanes = table.shape[1]
    steps = math.gcd(pool, 4)
    chunk = pool_rows // steps

    def whole(*shape):
        return pl.BlockSpec(shape, lambda step, _: (0,) * len(shape))

    piece = pl.BlockSpec((chunk, key_width), lambda step, _: (step, 0))
    shapes = [(kv_heads, HD, lanes), (kv_heads, 8, lanes), (slots.shape[0] * CAP * PAGE, lanes)]
    return pl.pallas_call(
        functools.partial(resident_kernel, group, pool),
        out_shape=tuple(jax.ShapeDtypeStruct(shape, jnp.float32) for shape in shapes),
        grid_spec=pltpu.PrefetchScalarGridSpec(
            num_scalar_prefetch=1,
            grid=(steps,),
            in_specs=[whole(*decode_query.shape), piece, piece]
            + [whole(*table.shape), whole(*lengths.shape)],
            out_specs=[whole(*shape) for shape in shapes],
            scratch_shapes=[pltpu.VMEM((chunk, lanes), jnp.float32)],
        ),
        compiler_params=params(60 * 2**20),
        cost_estimate=pl.CostEstimate(
            flops=6 * kv_heads * lanes * pool_rows * HD,
            bytes_accessed=4 * key_width * pool_rows,
            transcendentals=kv_heads * lanes * pool_rows,
        ),
        name="resident",
    )(slots, decode_query, keys, values, table, lengths)


def pages_here(ref, head, kv_heads, own, rows):
    codes = ref[rows:, :HD].astype(jnp.float32).astype(jnp.int32)
    found = []
    for slot in range(CAP):
        mine = codes == own * CAP + slot
        both = [jnp.zeros((PAGE, HD), jnp.float32)] * 2
        for page in range(rows // PAGE):
            here = jnp.broadcast_to(mine[page : page + 1], (PAGE, HD))
            cut = slice(page * PAGE, (page + 1) * PAGE)
            both = [
                jnp.where(here, ref[cut, c * HD : (c + 1) * HD].astype(jnp.float32), held)
                for c, held in zip((head, kv_heads + head), both)
            ]
        found.append(jnp.concatenate(both, axis=1))
    return jnp.concatenate(found, axis=0).astype(jnp.bfloat16)


def attend_kernel(n_blocks, n_pages, kv_heads, group, first, final, place_ref, *refs):
    refs = list(refs)

    def take(count):
        taken, refs[:count] = refs[:count], []
        return taken

    (query_ref,) = take(1)
    blocks = take(n_blocks)
    if not first:
        acc_in, stat_in = take(2)
    if final:
        decode_ref, side_acc, side_stat, bias_ref = take(4)
        pages = take(n_pages)
        out_ref, decode_out = refs
    else:
        acc_out, stat_out, page_out = refs
    rows = query_ref.shape[0]
    own = place_ref[0]
    seen = [place_ref[1 + b] < own for b in range(n_blocks)]

    def columns(ref, first_head, count=1):
        return ref[:rows, first_head * HD : (first_head + count) * HD]

    def score(head):
        keys = jnp.concatenate([columns(ref, head) for ref in blocks], axis=0)
        queries = jnp.concatenate(
            [columns(query_ref, head * group + h) for h in range(group)], axis=0
        )
        return lax.dot_general(keys, queries, NT, preferred_element_type=jnp.float32)

    def weigh(head, scores):
        pieces = [scores[b * rows : (b + 1) * rows] for b in range(n_blocks)]
        if first:
            key_of = lax.broadcasted_iota(jnp.int32, (rows, rows), 0)
            row_of = lax.broadcasted_iota(jnp.int32, (rows, rows), 1)
            kept = jnp.concatenate([key_of <= row_of] * group, axis=1)
            pieces[0] = jnp.where(kept, pieces[0], LOW)
            new_max = jnp.max(pieces[0], axis=0, keepdims=True)
        else:
            new_max = stat_in[head, 0:1]
        for b in range(1 if first else 0, n_blocks):
            highest = jnp.max(pieces[b], axis=0, keepdims=True)
            new_max = jnp.maximum(new_max, jnp.where(seen[b], highest, LOW))
        weights = []
        for b in range(n_blocks):
            shift = new_max
            if not (first and b == 0):
                shift = new_max + jnp.where(seen[b], 0.0, -LOW)
            weights.append(jnp.exp2(pieces[b] - shift).astype(jnp.bfloat16))
        return new_max, jnp.concatenate(weights, axis=0)

    def finish(head, new_max, weights):
        values = jnp.concatenate([columns(ref, kv_heads + head) for ref in blocks], axis=0)
        product = jnp.dot(
            turned_with_ones(values), weights, preferred_element_type=jnp.float32
        )
        acc, total = product[:HD], product[HD : HD + 1]
        if not first:
            fade = jnp.exp2(stat_in[head, 0:1] - new_max)
            acc += acc_in[head] * fade
            total += stat_in[head, 1:2] * fade
        if not final:
            acc_out[head] = acc
            stat_out[head, 0:1] = new_max
            stat_out[head, 1:2] = total
            return
        result = (acc * (1.0 / total)).astype(jnp.bfloat16)
        for h in range(group):
            out_ref[:, (head * group + h) * HD : (head * group + h + 1) * HD] = (
                result[:, h * rows : (h + 1) * rows].T
            )

    def incoming(head):
        return jnp.concatenate(
            [pages_here(ref, head, kv_heads, own, rows) for ref in blocks], axis=0
        )

    def decode(head):
        all_pages = jnp.concatenate([ref[head] for ref in pages] + [incoming(head)], axis=0)
        decode_rows = decode_ref.shape[0]
        queries = jnp.concatenate(
            [
                decode_ref[:, (head * group + h) * HD : (head * group + h + 1) * HD]
                for h in range(group)
            ],
            axis=0,
        )
        side_max = side_stat[head, 0:1]
        new_max, product = counted_piece(
            queries,
            all_pages[:, :HD],
            turned_with_ones(all_pages[:, HD:]),
            1.0,
            bias_ref[...],
            side_max,
        )
        fade = jnp.exp2(side_max - new_max)
        acc = product[:HD] + side_acc[head] * fade
        total = product[HD : HD + 1] + side_stat[head, 1:2] * fade
        result = (acc / total).T.astype(jnp.bfloat16)
        for h in range(group):
            decode_out[:, (head * group + h) * HD : (head * group + h + 1) * HD] = result[
                h * decode_rows : (h + 1) * decode_rows
            ]

    scores, waiting = score(0), None
    for head in range(kv_heads):
        later = score(head + 1) if head + 1 < kv_heads else None
        ready = weigh(head, scores)
        if waiting is not None:
            finish(head - 1, *waiting)
        if final:
            decode(head)
        else:
            page_out[head] = incoming(head)
        scores, waiting = later, ready
    finish(kv_heads - 1, *waiting)


def attend(arrived, section, query, state, decode, kv_heads):
    blocks = [block for block, _ in arrived]
    place = jnp.stack([section] + [s.astype(jnp.int32) for _, s in arrived])
    n_blocks = len(blocks)
    rows, query_width = query.shape
    group = query_width // (kv_heads * HD)
    first, final = state is None, decode is not None
    total_rows = group * rows
    vmem = pl.BlockSpec(memory_space=pltpu.VMEM)
    operands = [query, *blocks]
    held = []
    if not first:
        acc, stats, held = state
        operands += [acc, stats]
    if final:
        operands += [*decode, *held]
        out_shape = (
            jax.ShapeDtypeStruct(query.shape, jnp.bfloat16),
            jax.ShapeDtypeStruct(decode[0].shape, jnp.bfloat16),
        )
    else:
        out_shape = (
            jax.ShapeDtypeStruct((kv_heads, HD, total_rows), jnp.float32),
            jax.ShapeDtypeStruct((kv_heads, 8, total_rows), jnp.float32),
            jax.ShapeDtypeStruct((kv_heads, n_blocks * CAP * PAGE, 2 * HD), jnp.bfloat16),
        )
    pairs = kv_heads * total_rows * n_blocks * rows
    result = pl.pallas_call(
        functools.partial(attend_kernel, n_blocks, len(held), kv_heads, group, first, final),
        out_shape=out_shape,
        in_specs=[pl.BlockSpec(memory_space=pltpu.SMEM)] + [vmem] * len(operands),
        out_specs=[vmem] * len(out_shape),
        compiler_params=params(),
        cost_estimate=pl.CostEstimate(
            flops=6 * pairs * HD,
            bytes_accessed=12 * kv_heads * total_rows * HD,
            transcendentals=pairs,
        ),
        name="attend",
    )(place, *operands)
    if final:
        return result
    return result[0], result[1], [*held, result[2]]


def fence(*arrays):
    return lax.optimization_barrier(arrays)


def grid_sections():
    here = lax.axis_index("section")
    z, column = here // 4, here % 4
    inner = (z == 1) | (z == 2)
    plane_a = jnp.bitwise_xor(z, 1)
    plane_f = jnp.where(inner, 3 - z, jnp.where(z == 0, 2, 1))
    plane_g = jnp.where(inner, jnp.bitwise_xor(3 - z, 1), 3 - z)
    order = [(z, 0), (z, 1), (z, 2), (plane_a, 0), (z, 3), (plane_a, 2), (plane_f, 0)]
    order += [(plane_a, 1), (plane_f, 2), (plane_g, 0), (plane_f, 1), (plane_g, 2), (plane_f, 3)]
    order += [(plane_g, 1), (plane_a, 3), (plane_g, 3)]
    return [plane * 4 + jnp.bitwise_xor(column, turn) for plane, turn in order]


def gather_rounds(own, sections, work):
    sections = iter(sections)

    def named(*blocks):
        return [(block, next(sections)) for block in blocks]

    def settle(moved, work, *kept):
        return fence(*moved, *kept, *work)[: len(moved) + len(kept)]

    size_z, size_y, size_x = 4, 2, 2
    z = lax.axis_index("section") // 4

    def index(zz, yy, xx):
        return (zz * size_y + yy) * size_x + xx

    def along_z(pairs):
        return [
            (index(a, yy, xx), index(b, yy, xx))
            for a, b in pairs
            for yy in range(size_y)
            for xx in range(size_x)
        ]

    every = [(zz, yy, xx) for zz in range(size_z) for yy in range(size_y) for xx in range(size_x)]
    swap_x = [(index(zz, yy, xx), index(zz, yy, 1 - xx)) for zz, yy, xx in every]
    swap_y = [(index(zz, yy, xx), index(zz, 1 - yy, xx)) for zz, yy, xx in every]
    ends = along_z([(0, 1), (1, 0), (2, 3), (3, 2)])
    middle = along_z([(1, 2), (2, 1)])
    outward = along_z([(1, 0), (2, 3)])
    inner = (z == 1) | (z == 2)

    def move(block, pairs):
        return lax.ppermute(block, "section", pairs)

    moved = move(own, swap_x), move(own, swap_y), move(own, ends), move(own, middle)
    own_x, own_y, a, b = settle(moved, work)
    work = yield named(own, own_x, own_y, a)
    moved = move(own_y, swap_x), move(a, swap_y), move(b, outward), move(a, middle)
    own_d, a_y, c, d, a, b = settle(moved, work, a, b)
    f = jnp.where(inner, b, c)
    work = yield named(own_d, a_y, f)
    either = jnp.where(inner, d, own_d)
    moved = move(a, swap_x), move(f, swap_y), move(either, ends), move(own_d, middle)
    a_x, f_y, e, b_in, f, d = settle(moved, work, f, d)
    g = jnp.where(inner, d, e)
    work = yield named(a_x, f_y, g)
    moved = move(f, swap_x), move(g, swap_y), move(b_in, outward), move(e, middle)
    f_x, g_y, c_in, d_in, g, a_x, b_in, e = settle(moved, work, g, a_x, b_in, e)
    f_d = jnp.where(inner, b_in, c_in)
    work = yield named(f_x, g_y, f_d)
    moved = move(g, swap_x), move(a_x, swap_y), move(d_in, outward)
    g_x, a_turn, e_in = settle(moved, work)
    a_d = jnp.where(inner, e, a_turn)
    g_d = jnp.where(inner, d_in, e_in)
    yield named(g_x, a_d, g_d)


def plain_sections(section_count, section, pool):
    every = [jnp.int32(s) for s in range(section_count)]
    return [jnp.where(s == section, -pool, s) for s in every]


def gather_plain(own, section_count):
    rows = own.shape[0]
    gathered = lax.all_gather(own, "section", axis=0, tiled=True)
    step = math.gcd(section_count, 4)
    for top in range(0, section_count, step):
        yield [
            (gathered[s * rows : (s + 1) * rows], jnp.int32(s)) for s in range(top, top + step)
        ]


def per_device(
    prefill_hidden,
    norm_gain,
    key_weight,
    value_weight,
    prefill_query,
    resident_keys,
    resident_values,
    decode_query,
    page_owner,
    block_table,
    context_len,
):
    section_count = lax.axis_size("section")
    tp_count = lax.axis_size("tp")
    section = lax.axis_index("section").astype(jnp.int32)
    tp = lax.axis_index("tp").astype(jnp.int32)
    rows = prefill_hidden.shape[0]
    key_width = key_weight.shape[1]
    kv_heads = key_width // HD
    group = prefill_query.shape[1] // key_width
    pool = resident_keys.shape[0]

    if tp_count == 2:
        other = lax.ppermute(prefill_hidden, "tp", [(0, 1), (1, 0)])
        parts, order = [prefill_hidden, other], jnp.stack([tp, 1 - tp])
    else:
        parts = [lax.all_gather(prefill_hidden, "tp", axis=1, tiled=True)]
        order = jnp.zeros((1,), jnp.int32)
    half = HD // 2
    frequency = jnp.exp(jnp.arange(half, dtype=jnp.float32) * (-2.0 * math.log(ROPE_THETA) / HD))
    positions = section * rows + jnp.arange(rows, dtype=jnp.int32)
    angles = positions.astype(jnp.float32)[:, None] * frequency[None, :]
    cosine, sine = jnp.cos(angles), jnp.sin(angles)
    cosine = EXP2_SCALE * jnp.concatenate([cosine, cosine], axis=1)
    sine = EXP2_SCALE * jnp.concatenate([-sine, sine], axis=1)

    key_near, value_near = stage(key_weight, value_weight)
    own = project(
        parts, order, norm_gain, key_near, value_near, cosine, sine, page_owner
    )

    own, block_table, context_len = fence(own, block_table, context_len)
    table = jnp.concatenate([block_table] * group, axis=0).T
    lengths = jnp.concatenate([context_len] * group)[None, :]
    if section_count == 16:
        sections = grid_sections()
    else:
        sections = [section] + plain_sections(section_count, section, pool)
    decode = (
        decode_query,
        *resident_attention(
            decode_query,
            resident_keys.reshape(pool * PAGE, key_width),
            resident_values.reshape(pool * PAGE, key_width),
            table,
            lengths,
            jnp.stack(sections).astype(jnp.int32),
            pool,
        ),
    )

    def step(arrived, state, last=False):
        return attend(arrived, section, prefill_query, state, decode if last else None, kv_heads)

    if section_count == 16:
        rounds = gather_rounds(own, sections, decode[1:])
        arrived, state = next(rounds), None
        for _ in range(4):
            state = step(arrived, state)
            arrived = rounds.send((state[0], state[1]))
        return step(arrived, state, True)
    state = step([(own, section)], None)
    rounds = list(gather_plain(own, section_count))
    for arrived in rounds[:-1]:
        state = step(arrived, state)
    return step(rounds[-1], state, True)


def solution(mesh):
    return jax.shard_map(
        per_device,
        mesh=mesh,
        in_specs=(
            P("section", "tp"),
            P(),
            P(None, "tp"),
            P(None, "tp"),
            P("section", "tp"),
            P("section", None, "tp"),
            P("section", None, "tp"),
            P("section", "tp"),
            P("section"),
            P("section", None),
            P("section"),
        ),
        out_specs=(P("section", "tp"), P("section", "tp")),
        check_vma=False,
    )
```

```python
import functools
import math

import jax
import jax.numpy as jnp
from jax import lax
from jax.experimental import pallas as pl
from jax.experimental.pallas import tpu as pltpu
from jax.sharding import PartitionSpec as P

HD = 128
PAGE = 16
CAP = 2
CUT = 1024
NORM_EPSILON = 1e-05
ROPE_THETA = 500000.0
LOW = -1e30
EXP2_SCALE = math.log2(math.e) / math.sqrt(HD)
VMEM_BYTES = 32 * 1024 * 1024
NT = (((1,), (1,)), ((), ()))


def params(limit=VMEM_BYTES):
    return pltpu.CompilerParams(vmem_limit_bytes=limit)


def stage_kernel(n_arrays, *refs):
    copies = [
        pltpu.make_async_copy(refs[i], refs[n_arrays + i], refs[2 * n_arrays].at[i])
        for i in range(n_arrays)
    ]
    for copy in copies:
        copy.start()
    for copy in copies:
        copy.wait()


def stage(*arrays):
    return pl.pallas_call(
        functools.partial(stage_kernel, len(arrays)),
        out_shape=tuple(jax.ShapeDtypeStruct(a.shape, a.dtype) for a in arrays),
        in_specs=[pl.BlockSpec(memory_space=pl.ANY)] * len(arrays),
        out_specs=[pl.BlockSpec(memory_space=pltpu.VMEM)] * len(arrays),
        scratch_shapes=[pltpu.SemaphoreType.DMA((len(arrays),))],
        compiler_params=params(),
        cost_estimate=pl.CostEstimate(
            flops=0, bytes_accessed=sum(2 * a.size * a.dtype.itemsize for a in arrays), transcendentals=0
        ),
        name="stage",
    )(*arrays)


def project_kernel(n_parts, chunk, order_ref, *refs):
    parts = refs[:n_parts]
    gain_ref, key_ref, value_ref, cos_ref, sin_ref, column_ref, row_ref = refs[n_parts:-2]
    out_ref, total_ref = refs[-2:]
    rows, part_width = parts[0].shape
    key_width = key_ref.shape[1]
    pages = column_ref.shape[0]
    earlier = lax.broadcasted_iota(jnp.int32, (pages, pages), 1) < lax.broadcasted_iota(
        jnp.int32, (pages, pages), 0
    )
    same = earlier & (column_ref[...] == row_ref[...])
    rank = jnp.sum(same.astype(jnp.float32), axis=1, keepdims=True)
    codes = column_ref[...].astype(jnp.float32) * CAP + rank
    out_ref[rows:] = jnp.broadcast_to(codes, (pages, 2 * key_width)).astype(jnp.bfloat16)
    squares = jnp.zeros((rows, HD), jnp.float32)
    for part in parts:
        for first in range(0, part_width, HD):
            piece = part[:, first : first + HD].astype(jnp.float32)
            squares += piece * piece
    squares = jnp.sum(squares, axis=1, keepdims=True)
    inverse = lax.rsqrt(squares * (1.0 / (part_width * n_parts)) + NORM_EPSILON)
    for index, part in enumerate(parts):
        base = order_ref[index] * part_width
        for first in range(0, part_width, chunk):
            where = pl.multiple_of(base + first, chunk)
            piece = part[:, first : first + chunk].astype(jnp.float32)
            normed = (piece * inverse * gain_ref[:, pl.ds(where, chunk)]).astype(jnp.bfloat16)
            keys = jnp.dot(
                normed, key_ref[pl.ds(where, chunk)], preferred_element_type=jnp.float32
            )
            values = jnp.dot(
                normed, value_ref[pl.ds(where, chunk)], preferred_element_type=jnp.float32
            )
            if index == 0 and first == 0:
                total_ref[:, :key_width] = keys
                total_ref[:, key_width:] = values
            else:
                total_ref[:, :key_width] += keys
                total_ref[:, key_width:] += values
    for head in range(key_width // HD):
        cut = slice(head * HD, (head + 1) * HD)
        raw = total_ref[:, cut]
        turned = raw * cos_ref[...] + pltpu.roll(raw, HD // 2, 1) * sin_ref[...]
        out_ref[:rows, cut] = turned.astype(jnp.bfloat16)
    out_ref[:rows, key_width:] = total_ref[:, key_width:].astype(jnp.bfloat16)


def project(parts, order, norm_gain, key_weight, value_weight, cosine, sine, page_owner):
    rows, part_width = parts[0].shape
    n_parts = len(parts)
    key_width = key_weight.shape[1]
    vmem = pl.BlockSpec(memory_space=pltpu.VMEM)
    pages = page_owner.shape[0]
    return pl.pallas_call(
        functools.partial(project_kernel, n_parts, math.gcd(part_width, 1024)),
        out_shape=jax.ShapeDtypeStruct((rows + pages, 2 * key_width), jnp.bfloat16),
        in_specs=[pl.BlockSpec(memory_space=pltpu.SMEM)] + [vmem] * (n_parts + 7),
        out_specs=vmem,
        scratch_shapes=[pltpu.VMEM((rows, 2 * key_width), jnp.float32)],
        compiler_params=params(),
        cost_estimate=pl.CostEstimate(
            flops=4 * rows * key_width * part_width * n_parts,
            bytes_accessed=4 * key_width * part_width * n_parts,
            transcendentals=0,
        ),
        name="project",
    )(
        order,
        *parts,
        norm_gain.reshape(1, -1),
        key_weight,
        value_weight,
        cosine,
        sine,
        page_owner.reshape(-1, 1),
        page_owner.reshape(1, -1),
    )


def turned_with_ones(values):
    turned = values.T
    return jnp.concatenate([turned, jnp.ones((16, turned.shape[1]), turned.dtype)], axis=0)


def counted_piece(queries, keys, values_ones, factor, bias, old_max):
    scores = lax.dot_general(keys, queries, NT, preferred_element_type=jnp.float32)
    scores = scores * factor + bias
    new_max = jnp.maximum(old_max, jnp.max(scores, axis=0, keepdims=True))
    weights = jnp.exp2(scores - new_max).astype(jnp.bfloat16)
    product = jnp.dot(values_ones, weights, preferred_element_type=jnp.float32)
    return new_max, product


def page_bias(ids, table_ref, length, store):
    pages, lanes = ids.shape
    found = jnp.zeros((pages, lanes), jnp.int32)
    for entry in range(table_ref.shape[0]):
        left = length - entry * PAGE
        weight = jnp.where(left >= PAGE, 1, jnp.where(left > 0, CUT, 0))
        found += jnp.where(ids == table_ref[entry : entry + 1, :], weight, 0)

    def logarithm(count):
        return jnp.where(count > 0, jnp.log2(jnp.maximum(count, 1).astype(jnp.float32)), LOW)

    whole = found & (CUT - 1)
    with_cut = logarithm(whole + lax.shift_right_logical(found, CUT.bit_length() - 1))
    whole = logarithm(whole)
    token = lax.broadcasted_iota(jnp.int32, (PAGE, lanes), 0)
    kept = token < length % PAGE
    for page in range(pages):
        one = slice(page, page + 1)
        store(page, jnp.where(kept, with_cut[one], whole[one]))


def resident_kernel(
    group, pool, slot_ref, query_ref, key_ref, value_ref, table_ref, length_ref, *refs
):
    acc_ref, stat_ref, slot_bias_ref, bias = refs
    step = pl.program_id(0)
    pages, lanes = bias.shape[0] // PAGE, bias.shape[1]

    @pl.when(step == 0)
    def _():
        acc_ref[...] = jnp.zeros_like(acc_ref)
        stat_ref[:, 0:1] = jnp.full_like(stat_ref[:, 0:1], LOW)
        stat_ref[:, 1:2] = jnp.zeros_like(stat_ref[:, 1:2])
        slots = slot_bias_ref.shape[0] // PAGE
        slot_of = lax.broadcasted_iota(jnp.int32, (slots, lanes), 0)
        ids = slot_of % CAP
        for block in range(slots // CAP):
            ids += jnp.where(slot_of // CAP == block, pool + slot_ref[block] * CAP, 0)

        def store_slot(page, found):
            slot_bias_ref[page * PAGE : (page + 1) * PAGE] = found

        page_bias(ids, table_ref, length_ref[...], store_slot)

    def store(page, found):
        bias[page * PAGE : (page + 1) * PAGE] = found

    ids = step * pages + lax.broadcasted_iota(jnp.int32, (pages, lanes), 0)
    page_bias(ids, table_ref, length_ref[...], store)
    for head in range(key_ref.shape[1] // HD):
        cut = slice(head * HD, (head + 1) * HD)
        queries = jnp.concatenate(
            [
                query_ref[:, (head * group + h) * HD : (head * group + h + 1) * HD]
                for h in range(group)
            ],
            axis=0,
        )
        old_max = stat_ref[head, 0:1]
        new_max, product = counted_piece(
            queries,
            key_ref[:, cut],
            turned_with_ones(value_ref[:, cut]),
            EXP2_SCALE,
            bias[...],
            old_max,
        )
        fade = jnp.exp2(old_max - new_max)
        acc_ref[head] = acc_ref[head] * fade + product[:HD]
        stat_ref[head, 1:2] = stat_ref[head, 1:2] * fade + product[HD : HD + 1]
        stat_ref[head, 0:1] = new_max


def resident_attention(decode_query, keys, values, table, lengths, slots, pool):
    pool_rows, key_width = keys.shape
    kv_heads = key_width // HD
    group = decode_query.shape[1] // key_width
    lanes = table.shape[1]
    steps = math.gcd(pool, 4)
    chunk = pool_rows // steps

    def whole(*shape):
        return pl.BlockSpec(shape, lambda step, _: (0,) * len(shape))

    piece = pl.BlockSpec((chunk, key_width), lambda step, _: (step, 0))
    shapes = [(kv_heads, HD, lanes), (kv_heads, 8, lanes), (slots.shape[0] * CAP * PAGE, lanes)]
    return pl.pallas_call(
        functools.partial(resident_kernel, group, pool),
        out_shape=tuple(jax.ShapeDtypeStruct(shape, jnp.float32) for shape in shapes),
        grid_spec=pltpu.PrefetchScalarGridSpec(
            num_scalar_prefetch=1,
            grid=(steps,),
            in_specs=[whole(*decode_query.shape), piece, piece]
            + [whole(*table.shape), whole(*lengths.shape)],
            out_specs=[whole(*shape) for shape in shapes],
            scratch_shapes=[pltpu.VMEM((chunk, lanes), jnp.float32)],
        ),
        compiler_params=params(60 * 2**20),
        cost_estimate=pl.CostEstimate(
            flops=6 * kv_heads * lanes * pool_rows * HD,
            bytes_accessed=4 * key_width * pool_rows,
            transcendentals=kv_heads * lanes * pool_rows,
        ),
        name="resident",
    )(slots, decode_query, keys, values, table, lengths)


def pages_here(ref, head, kv_heads, own, rows, lanes):
    codes = ref[rows:, :HD].astype(jnp.float32).astype(jnp.int32)
    found = []
    for slot in range(CAP):
        mine = codes == own * CAP + slot
        both = [jnp.zeros((PAGE, HD), jnp.float32)] * 2
        for page in range(rows // PAGE):
            here = jnp.broadcast_to(mine[page : page + 1], (PAGE, HD))
            cut = slice(page * PAGE, (page + 1) * PAGE)
            both = [
                jnp.where(here, ref[cut, lanes(c)].astype(jnp.float32), held)
                for c, held in zip((head, kv_heads + head), both)
            ]
        found.append(jnp.concatenate(both, axis=1))
    return jnp.concatenate(found, axis=0).astype(jnp.bfloat16)


def attend_kernel(n_blocks, n_pages, kv_heads, group, unroll, first, final, place_ref, *refs):
    refs = list(refs)

    def take(count):
        taken, refs[:count] = refs[:count], []
        return taken

    (query_ref,) = take(1)
    blocks = take(n_blocks)
    if not first:
        acc_in, stat_in = take(2)
    if final:
        decode_ref, side_acc, side_stat, bias_ref = take(4)
        pages = take(n_pages)
        out_ref, decode_out = refs
    else:
        acc_out, stat_out, page_out = refs
    rows = query_ref.shape[0]
    own = place_ref[0]
    seen = [place_ref[1 + b] < own for b in range(n_blocks)]

    first_head = pl.program_id(0) * unroll

    def lanes(head):
        return pl.ds(pl.multiple_of(head * HD, HD), HD)

    def columns(ref, head):
        return ref[:rows, lanes(head)]

    def score(head):
        keys = jnp.concatenate([columns(ref, head) for ref in blocks], axis=0)
        queries = jnp.concatenate(
            [columns(query_ref, head * group + h) for h in range(group)], axis=0
        )
        return lax.dot_general(keys, queries, NT, preferred_element_type=jnp.float32)

    def weigh(head, scores):
        pieces = [scores[b * rows : (b + 1) * rows] for b in range(n_blocks)]
        if first:
            key_of = lax.broadcasted_iota(jnp.int32, (rows, rows), 0)
            row_of = lax.broadcasted_iota(jnp.int32, (rows, rows), 1)
            kept = jnp.concatenate([key_of <= row_of] * group, axis=1)
            pieces[0] = jnp.where(kept, pieces[0], LOW)
            new_max = jnp.max(pieces[0], axis=0, keepdims=True)
        else:
            new_max = stat_in[head, 0:1]
        for b in range(1 if first else 0, n_blocks):
            highest = jnp.max(pieces[b], axis=0, keepdims=True)
            new_max = jnp.maximum(new_max, jnp.where(seen[b], highest, LOW))
        weights = []
        for b in range(n_blocks):
            shift = new_max
            if not (first and b == 0):
                shift = new_max + jnp.where(seen[b], 0.0, -LOW)
            weights.append(jnp.exp2(pieces[b] - shift).astype(jnp.bfloat16))
        return new_max, jnp.concatenate(weights, axis=0)

    def finish(head, new_max, weights):
        values = jnp.concatenate([columns(ref, kv_heads + head) for ref in blocks], axis=0)
        product = jnp.dot(
            turned_with_ones(values), weights, preferred_element_type=jnp.float32
        )
        acc, total = product[:HD], product[HD : HD + 1]
        if not first:
            fade = jnp.exp2(stat_in[head, 0:1] - new_max)
            acc += acc_in[head] * fade
            total += stat_in[head, 1:2] * fade
        if not final:
            acc_out[head] = acc
            stat_out[head, 0:1] = new_max
            stat_out[head, 1:2] = total
            return
        result = (acc * (1.0 / total)).astype(jnp.bfloat16)
        for h in range(group):
            out_ref[:, lanes(head * group + h)] = (
                result[:, h * rows : (h + 1) * rows].T
            )

    def incoming(head):
        return jnp.concatenate(
            [pages_here(ref, head, kv_heads, own, rows, lanes) for ref in blocks], axis=0
        )

    def decode(head):
        all_pages = jnp.concatenate([ref[head] for ref in pages] + [incoming(head)], axis=0)
        decode_rows = decode_ref.shape[0]
        queries = jnp.concatenate(
            [decode_ref[:, lanes(head * group + h)] for h in range(group)], axis=0
        )
        side_max = side_stat[head, 0:1]
        new_max, product = counted_piece(
            queries,
            all_pages[:, :HD],
            turned_with_ones(all_pages[:, HD:]),
            1.0,
            bias_ref[...],
            side_max,
        )
        fade = jnp.exp2(side_max - new_max)
        acc = product[:HD] + side_acc[head] * fade
        total = product[HD : HD + 1] + side_stat[head, 1:2] * fade
        result = (acc / total).T.astype(jnp.bfloat16)
        for h in range(group):
            decode_out[:, lanes(head * group + h)] = result[h * decode_rows : (h + 1) * decode_rows]

    scores, waiting = score(first_head), None
    for index in range(unroll):
        head = first_head + index
        later = score(head + 1) if index + 1 < unroll else None
        ready = weigh(head, scores)
        if waiting is not None:
            finish(head - 1, *waiting)
        if final:
            decode(head)
        else:
            page_out[head] = incoming(head)
        scores, waiting = later, ready
    finish(first_head + unroll - 1, *waiting)


def attend(arrived, section, query, state, decode, kv_heads):
    blocks = [block for block, _ in arrived]
    place = jnp.stack([section] + [s.astype(jnp.int32) for _, s in arrived])
    n_blocks = len(blocks)
    rows, query_width = query.shape
    group = query_width // (kv_heads * HD)
    first, final = state is None, decode is not None
    total_rows = group * rows
    unroll = math.gcd(kv_heads, 2)
    vmem = pl.BlockSpec(memory_space=pltpu.VMEM)
    operands = [query, *blocks]
    held = []
    if not first:
        acc, stats, held = state
        operands += [acc, stats]
    if final:
        operands += [*decode, *held]
        out_shape = (
            jax.ShapeDtypeStruct(query.shape, jnp.bfloat16),
            jax.ShapeDtypeStruct(decode[0].shape, jnp.bfloat16),
        )
    else:
        out_shape = (
            jax.ShapeDtypeStruct((kv_heads, HD, total_rows), jnp.float32),
            jax.ShapeDtypeStruct((kv_heads, 8, total_rows), jnp.float32),
            jax.ShapeDtypeStruct((kv_heads, n_blocks * CAP * PAGE, 2 * HD), jnp.bfloat16),
        )
    pairs = kv_heads * total_rows * n_blocks * rows
    result = pl.pallas_call(
        functools.partial(
            attend_kernel, n_blocks, len(held), kv_heads, group, unroll, first, final
        ),
        out_shape=out_shape,
        grid=(kv_heads // unroll,),
        in_specs=[pl.BlockSpec(memory_space=pltpu.SMEM)] + [vmem] * len(operands),
        out_specs=[vmem] * len(out_shape),
        compiler_params=params(),
        cost_estimate=pl.CostEstimate(
            flops=6 * pairs * HD,
            bytes_accessed=12 * kv_heads * total_rows * HD,
            transcendentals=pairs,
        ),
        name="attend",
    )(place, *operands)
    if final:
        return result
    return result[0], result[1], [*held, result[2]]


def fence(*arrays):
    return lax.optimization_barrier(arrays)


def grid_sections():
    here = lax.axis_index("section")
    z, column = here // 4, here % 4
    inner = (z == 1) | (z == 2)
    plane_a = jnp.bitwise_xor(z, 1)
    plane_f = jnp.where(inner, 3 - z, jnp.where(z == 0, 2, 1))
    plane_g = jnp.where(inner, jnp.bitwise_xor(3 - z, 1), 3 - z)
    order = [(z, 0), (z, 1), (z, 2), (plane_a, 0), (z, 3), (plane_a, 2), (plane_f, 0)]
    order += [(plane_a, 1), (plane_f, 2), (plane_g, 0), (plane_f, 1), (plane_g, 2), (plane_f, 3)]
    order += [(plane_g, 1), (plane_a, 3), (plane_g, 3)]
    return [plane * 4 + jnp.bitwise_xor(column, turn) for plane, turn in order]


def gather_rounds(own, sections, work):
    sections = iter(sections)

    def named(*blocks):
        return [(block, next(sections)) for block in blocks]

    def settle(moved, work, *kept):
        return fence(*moved, *kept, *work)[: len(moved) + len(kept)]

    size_z, size_y, size_x = 4, 2, 2
    z = lax.axis_index("section") // 4

    def index(zz, yy, xx):
        return (zz * size_y + yy) * size_x + xx

    def along_z(pairs):
        return [
            (index(a, yy, xx), index(b, yy, xx))
            for a, b in pairs
            for yy in range(size_y)
            for xx in range(size_x)
        ]

    every = [(zz, yy, xx) for zz in range(size_z) for yy in range(size_y) for xx in range(size_x)]
    swap_x = [(index(zz, yy, xx), index(zz, yy, 1 - xx)) for zz, yy, xx in every]
    swap_y = [(index(zz, yy, xx), index(zz, 1 - yy, xx)) for zz, yy, xx in every]
    ends = along_z([(0, 1), (1, 0), (2, 3), (3, 2)])
    middle = along_z([(1, 2), (2, 1)])
    outward = along_z([(1, 0), (2, 3)])
    inner = (z == 1) | (z == 2)

    def move(block, pairs):
        return lax.ppermute(block, "section", pairs)

    moved = move(own, swap_x), move(own, swap_y), move(own, ends), move(own, middle)
    own_x, own_y, a, b = settle(moved, work)
    work = yield named(own, own_x, own_y, a)
    moved = move(own_y, swap_x), move(a, swap_y), move(b, outward), move(a, middle)
    own_d, a_y, c, d, a, b = settle(moved, work, a, b)
    f = jnp.where(inner, b, c)
    work = yield named(own_d, a_y, f)
    either = jnp.where(inner, d, own_d)
    moved = move(a, swap_x), move(f, swap_y), move(either, ends), move(own_d, middle)
    a_x, f_y, e, b_in, f, d = settle(moved, work, f, d)
    g = jnp.where(inner, d, e)
    work = yield named(a_x, f_y, g)
    moved = move(f, swap_x), move(g, swap_y), move(b_in, outward), move(e, middle)
    f_x, g_y, c_in, d_in, g, a_x, b_in, e = settle(moved, work, g, a_x, b_in, e)
    f_d = jnp.where(inner, b_in, c_in)
    work = yield named(f_x, g_y, f_d)
    moved = move(g, swap_x), move(a_x, swap_y), move(d_in, outward)
    g_x, a_turn, e_in = settle(moved, work)
    a_d = jnp.where(inner, e, a_turn)
    g_d = jnp.where(inner, d_in, e_in)
    yield named(g_x, a_d, g_d)


def plain_sections(section_count, section, pool):
    every = [jnp.int32(s) for s in range(section_count)]
    return [jnp.where(s == section, -pool, s) for s in every]


def gather_plain(own, section_count):
    rows = own.shape[0]
    gathered = lax.all_gather(own, "section", axis=0, tiled=True)
    step = math.gcd(section_count, 4)
    for top in range(0, section_count, step):
        yield [
            (gathered[s * rows : (s + 1) * rows], jnp.int32(s)) for s in range(top, top + step)
        ]


def per_device(
    prefill_hidden,
    norm_gain,
    key_weight,
    value_weight,
    prefill_query,
    resident_keys,
    resident_values,
    decode_query,
    page_owner,
    block_table,
    context_len,
):
    section_count = lax.axis_size("section")
    tp_count = lax.axis_size("tp")
    section = lax.axis_index("section").astype(jnp.int32)
    tp = lax.axis_index("tp").astype(jnp.int32)
    rows = prefill_hidden.shape[0]
    key_width = key_weight.shape[1]
    kv_heads = key_width // HD
    group = prefill_query.shape[1] // key_width
    pool = resident_keys.shape[0]

    if tp_count == 2:
        other = lax.ppermute(prefill_hidden, "tp", [(0, 1), (1, 0)])
        parts, order = [prefill_hidden, other], jnp.stack([tp, 1 - tp])
    else:
        parts = [lax.all_gather(prefill_hidden, "tp", axis=1, tiled=True)]
        order = jnp.zeros((1,), jnp.int32)
    half = HD // 2
    frequency = jnp.exp(jnp.arange(half, dtype=jnp.float32) * (-2.0 * math.log(ROPE_THETA) / HD))
    positions = section * rows + jnp.arange(rows, dtype=jnp.int32)
    angles = positions.astype(jnp.float32)[:, None] * frequency[None, :]
    cosine, sine = jnp.cos(angles), jnp.sin(angles)
    cosine = EXP2_SCALE * jnp.concatenate([cosine, cosine], axis=1)
    sine = EXP2_SCALE * jnp.concatenate([-sine, sine], axis=1)

    key_near, value_near = stage(key_weight, value_weight)
    own = project(
        parts, order, norm_gain, key_near, value_near, cosine, sine, page_owner
    )

    own, block_table, context_len = fence(own, block_table, context_len)
    table = jnp.concatenate([block_table] * group, axis=0).T
    lengths = jnp.concatenate([context_len] * group)[None, :]
    if section_count == 16:
        sections = grid_sections()
    else:
        sections = [section] + plain_sections(section_count, section, pool)
    decode = (
        decode_query,
        *resident_attention(
            decode_query,
            resident_keys.reshape(pool * PAGE, key_width),
            resident_values.reshape(pool * PAGE, key_width),
            table,
            lengths,
            jnp.stack(sections).astype(jnp.int32),
            pool,
        ),
    )

    def step(arrived, state, last=False):
        return attend(arrived, section, prefill_query, state, decode if last else None, kv_heads)

    if section_count == 16:
        rounds = gather_rounds(own, sections, decode[1:])
        arrived, state = next(rounds), None
        for _ in range(4):
            state = step(arrived, state)
            arrived = rounds.send((state[0], state[1]))
        return step(arrived, state, True)
    state = step([(own, section)], None)
    rounds = list(gather_plain(own, section_count))
    for arrived in rounds[:-1]:
        state = step(arrived, state)
    return step(rounds[-1], state, True)


def solution(mesh):
    return jax.shard_map(
        per_device,
        mesh=mesh,
        in_specs=(
            P("section", "tp"),
            P(),
            P(None, "tp"),
            P(None, "tp"),
            P("section", "tp"),
            P("section", None, "tp"),
            P("section", None, "tp"),
            P("section", "tp"),
            P("section"),
            P("section", None),
            P("section"),
        ),
        out_specs=(P("section", "tp"), P("section", "tp")),
        check_vma=False,
    )
```

```python
import functools
import math

import jax
import jax.numpy as jnp
from jax import lax
from jax.experimental import pallas as pl
from jax.experimental.pallas import tpu as pltpu
from jax.sharding import PartitionSpec as P

HD = 128
PAGE = 16
CAP = 2
CUT = 1024
NORM_EPSILON = 1e-05
ROPE_THETA = 500000.0
LOW = -1e30
EXP2_SCALE = math.log2(math.e) / math.sqrt(HD)
VMEM_BYTES = 32 * 1024 * 1024
NT = (((1,), (1,)), ((), ()))


def params(limit=VMEM_BYTES):
    return pltpu.CompilerParams(vmem_limit_bytes=limit)


def stage_kernel(n_arrays, *refs):
    copies = [
        pltpu.make_async_copy(refs[i], refs[n_arrays + i], refs[2 * n_arrays].at[i])
        for i in range(n_arrays)
    ]
    for copy in copies:
        copy.start()
    for copy in copies:
        copy.wait()


def stage(*arrays):
    return pl.pallas_call(
        functools.partial(stage_kernel, len(arrays)),
        out_shape=tuple(jax.ShapeDtypeStruct(a.shape, a.dtype) for a in arrays),
        in_specs=[pl.BlockSpec(memory_space=pl.ANY)] * len(arrays),
        out_specs=[pl.BlockSpec(memory_space=pltpu.VMEM)] * len(arrays),
        scratch_shapes=[pltpu.SemaphoreType.DMA((len(arrays),))],
        compiler_params=params(),
        cost_estimate=pl.CostEstimate(
            flops=0, bytes_accessed=sum(2 * a.size * a.dtype.itemsize for a in arrays), transcendentals=0
        ),
        name="stage",
    )(*arrays)


def project_kernel(n_parts, chunk, order_ref, *refs):
    parts = refs[:n_parts]
    gain_ref, key_ref, value_ref, cos_ref, sin_ref, owner_ref = refs[n_parts:-2]
    out_ref, total_ref = refs[-2:]
    rows, part_width = parts[0].shape
    key_width = key_ref.shape[1]
    pages = owner_ref.shape[1]
    down = lax.broadcasted_iota(jnp.int32, (pages, pages), 0)
    along = lax.broadcasted_iota(jnp.int32, (pages, pages), 1)
    owners = jnp.broadcast_to(owner_ref[...].astype(jnp.float32), (pages, pages))
    column = jnp.sum(jnp.where(down == along, owners, 0.0), axis=1, keepdims=True)
    same = (along < down) & (column == owners)
    rank = jnp.sum(same.astype(jnp.float32), axis=1, keepdims=True)
    codes = column * CAP + rank
    out_ref[rows:] = jnp.broadcast_to(codes, (pages, 2 * key_width)).astype(jnp.bfloat16)
    squares = jnp.zeros((rows, HD), jnp.float32)
    for part in parts:
        for first in range(0, part_width, HD):
            piece = part[:, first : first + HD].astype(jnp.float32)
            squares += piece * piece
    squares = jnp.sum(squares, axis=1, keepdims=True)
    inverse = lax.rsqrt(squares * (1.0 / (part_width * n_parts)) + NORM_EPSILON)
    for index, part in enumerate(parts):
        base = order_ref[index] * part_width
        for first in range(0, part_width, chunk):
            where = pl.multiple_of(base + first, chunk)
            piece = part[:, first : first + chunk].astype(jnp.float32)
            normed = (piece * inverse * gain_ref[:, pl.ds(where, chunk)]).astype(jnp.bfloat16)
            keys = jnp.dot(
                normed, key_ref[pl.ds(where, chunk)], preferred_element_type=jnp.float32
            )
            values = jnp.dot(
                normed, value_ref[pl.ds(where, chunk)], preferred_element_type=jnp.float32
            )
            if index == 0 and first == 0:
                total_ref[:, :key_width] = keys
                total_ref[:, key_width:] = values
            else:
                total_ref[:, :key_width] += keys
                total_ref[:, key_width:] += values
    for head in range(key_width // HD):
        cut = slice(head * HD, (head + 1) * HD)
        raw = total_ref[:, cut]
        turned = raw * cos_ref[...] + pltpu.roll(raw, HD // 2, 1) * sin_ref[...]
        out_ref[:rows, cut] = turned.astype(jnp.bfloat16)
    out_ref[:rows, key_width:] = total_ref[:, key_width:].astype(jnp.bfloat16)


def project(parts, order, norm_gain, key_weight, value_weight, cosine, sine, page_owner):
    rows, part_width = parts[0].shape
    n_parts = len(parts)
    key_width = key_weight.shape[1]
    vmem = pl.BlockSpec(memory_space=pltpu.VMEM)
    pages = page_owner.shape[0]
    return pl.pallas_call(
        functools.partial(project_kernel, n_parts, math.gcd(part_width, 1024)),
        out_shape=jax.ShapeDtypeStruct((rows + pages, 2 * key_width), jnp.bfloat16),
        in_specs=[pl.BlockSpec(memory_space=pltpu.SMEM)] + [vmem] * (n_parts + 6),
        out_specs=vmem,
        scratch_shapes=[pltpu.VMEM((rows, 2 * key_width), jnp.float32)],
        compiler_params=params(),
        cost_estimate=pl.CostEstimate(
            flops=4 * rows * key_width * part_width * n_parts,
            bytes_accessed=4 * key_width * part_width * n_parts,
            transcendentals=0,
        ),
        name="project",
    )(
        order,
        *parts,
        norm_gain.reshape(1, -1),
        key_weight,
        value_weight,
        cosine,
        sine,
        page_owner.reshape(1, -1),
    )


def turned_with_ones(values):
    turned = values.T
    return jnp.concatenate([turned, jnp.ones((16, turned.shape[1]), turned.dtype)], axis=0)


def counted_piece(queries, keys, values_ones, factor, bias, old_max):
    scores = lax.dot_general(keys, queries, NT, preferred_element_type=jnp.float32)
    scores = scores * factor + bias
    new_max = jnp.maximum(old_max, jnp.max(scores, axis=0, keepdims=True))
    weights = jnp.exp2(scores - new_max).astype(jnp.bfloat16)
    product = jnp.dot(values_ones, weights, preferred_element_type=jnp.float32)
    return new_max, product


def page_bias(ids, table_ref, length, store):
    pages, lanes = ids.shape
    found = jnp.zeros((pages, lanes), jnp.int32)
    for entry in range(table_ref.shape[0]):
        left = length - entry * PAGE
        weight = jnp.where(left >= PAGE, 1, jnp.where(left > 0, CUT, 0))
        found += jnp.where(ids == table_ref[entry : entry + 1, :], weight, 0)

    def logarithm(count):
        return jnp.where(count > 0, jnp.log2(jnp.maximum(count, 1).astype(jnp.float32)), LOW)

    whole = found & (CUT - 1)
    with_cut = logarithm(whole + lax.shift_right_logical(found, CUT.bit_length() - 1))
    whole = logarithm(whole)
    token = lax.broadcasted_iota(jnp.int32, (PAGE, lanes), 0)
    kept = token < length % PAGE
    for page in range(pages):
        one = slice(page, page + 1)
        store(page, jnp.where(kept, with_cut[one], whole[one]))


def resident_kernel(
    group, pool, slot_ref, query_ref, key_ref, value_ref, table_ref, length_ref, *refs
):
    acc_ref, stat_ref, slot_bias_ref, bias = refs
    step = pl.program_id(0)
    pages, lanes = bias.shape[0] // PAGE, bias.shape[1]

    @pl.when(step == 0)
    def _():
        acc_ref[...] = jnp.zeros_like(acc_ref)
        stat_ref[:, 0:1] = jnp.full_like(stat_ref[:, 0:1], LOW)
        stat_ref[:, 1:2] = jnp.zeros_like(stat_ref[:, 1:2])
        slots = slot_bias_ref.shape[0] // PAGE
        slot_of = lax.broadcasted_iota(jnp.int32, (slots, lanes), 0)
        ids = slot_of % CAP
        for block in range(slots // CAP):
            ids += jnp.where(slot_of // CAP == block, pool + slot_ref[block] * CAP, 0)

        def store_slot(page, found):
            slot_bias_ref[page * PAGE : (page + 1) * PAGE] = found

        page_bias(ids, table_ref, length_ref[...], store_slot)

    def store(page, found):
        bias[page * PAGE : (page + 1) * PAGE] = found

    ids = step * pages + lax.broadcasted_iota(jnp.int32, (pages, lanes), 0)
    page_bias(ids, table_ref, length_ref[...], store)
    for head in range(key_ref.shape[1] // HD):
        cut = slice(head * HD, (head + 1) * HD)
        queries = jnp.concatenate(
            [
                query_ref[:, (head * group + h) * HD : (head * group + h + 1) * HD]
                for h in range(group)
            ],
            axis=0,
        )
        old_max = stat_ref[head, 0:1]
        new_max, product = counted_piece(
            queries,
            key_ref[:, cut],
            turned_with_ones(value_ref[:, cut]),
            EXP2_SCALE,
            bias[...],
            old_max,
        )
        fade = jnp.exp2(old_max - new_max)
        acc_ref[head] = acc_ref[head] * fade + product[:HD]
        stat_ref[head, 1:2] = stat_ref[head, 1:2] * fade + product[HD : HD + 1]
        stat_ref[head, 0:1] = new_max


def resident_attention(decode_query, keys, values, table, lengths, slots, pool):
    pool_rows, key_width = keys.shape
    kv_heads = key_width // HD
    group = decode_query.shape[1] // key_width
    lanes = table.shape[1]
    steps = math.gcd(pool, 4)
    chunk = pool_rows // steps

    def whole(*shape):
        return pl.BlockSpec(shape, lambda step, _: (0,) * len(shape))

    piece = pl.BlockSpec((chunk, key_width), lambda step, _: (step, 0))
    shapes = [(kv_heads, HD, lanes), (kv_heads, 8, lanes), (slots.shape[0] * CAP * PAGE, lanes)]
    return pl.pallas_call(
        functools.partial(resident_kernel, group, pool),
        out_shape=tuple(jax.ShapeDtypeStruct(shape, jnp.float32) for shape in shapes),
        grid_spec=pltpu.PrefetchScalarGridSpec(
            num_scalar_prefetch=1,
            grid=(steps,),
            in_specs=[whole(*decode_query.shape), piece, piece]
            + [whole(*table.shape), whole(*lengths.shape)],
            out_specs=[whole(*shape) for shape in shapes],
            scratch_shapes=[pltpu.VMEM((chunk, lanes), jnp.float32)],
        ),
        compiler_params=params(60 * 2**20),
        cost_estimate=pl.CostEstimate(
            flops=6 * kv_heads * lanes * pool_rows * HD,
            bytes_accessed=4 * key_width * pool_rows,
            transcendentals=kv_heads * lanes * pool_rows,
        ),
        name="resident",
    )(slots, decode_query, keys, values, table, lengths)


def pages_here(ref, head, kv_heads, own, rows, lanes):
    codes = ref[rows:, :HD].astype(jnp.float32).astype(jnp.int32)
    found = []
    for slot in range(CAP):
        mine = codes == own * CAP + slot
        both = [jnp.zeros((PAGE, HD), jnp.float32)] * 2
        for page in range(rows // PAGE):
            here = jnp.broadcast_to(mine[page : page + 1], (PAGE, HD))
            cut = slice(page * PAGE, (page + 1) * PAGE)
            both = [
                jnp.where(here, ref[cut, lanes(c)].astype(jnp.float32), held)
                for c, held in zip((head, kv_heads + head), both)
            ]
        found.append(jnp.concatenate(both, axis=1))
    return jnp.concatenate(found, axis=0).astype(jnp.bfloat16)


def attend_kernel(n_blocks, n_pages, kv_heads, group, unroll, first, final, place_ref, *refs):
    refs = list(refs)

    def take(count):
        taken, refs[:count] = refs[:count], []
        return taken

    (query_ref,) = take(1)
    blocks = take(n_blocks)
    if not first:
        acc_in, stat_in = take(2)
    if final:
        decode_ref, side_acc, side_stat, bias_ref = take(4)
        pages = take(n_pages)
        out_ref, decode_out = refs
    else:
        acc_out, stat_out, page_out = refs
    rows = query_ref.shape[0]
    own = place_ref[0]
    seen = [place_ref[1 + b] < own for b in range(n_blocks)]

    first_head = pl.program_id(0) * unroll

    def lanes(head):
        return pl.ds(pl.multiple_of(head * HD, HD), HD)

    def columns(ref, head):
        return ref[:rows, lanes(head)]

    def score(head):
        keys = jnp.concatenate([columns(ref, head) for ref in blocks], axis=0)
        queries = jnp.concatenate(
            [columns(query_ref, head * group + h) for h in range(group)], axis=0
        )
        return lax.dot_general(keys, queries, NT, preferred_element_type=jnp.float32)

    def weigh(head, scores):
        pieces = [scores[b * rows : (b + 1) * rows] for b in range(n_blocks)]
        if first:
            key_of = lax.broadcasted_iota(jnp.int32, (rows, rows), 0)
            row_of = lax.broadcasted_iota(jnp.int32, (rows, rows), 1)
            kept = jnp.concatenate([key_of <= row_of] * group, axis=1)
            pieces[0] = jnp.where(kept, pieces[0], LOW)
            new_max = jnp.max(pieces[0], axis=0, keepdims=True)
        else:
            new_max = stat_in[head, 0:1]
        for b in range(1 if first else 0, n_blocks):
            highest = jnp.max(pieces[b], axis=0, keepdims=True)
            new_max = jnp.maximum(new_max, jnp.where(seen[b], highest, LOW))
        weights = []
        for b in range(n_blocks):
            shift = new_max
            if not (first and b == 0):
                shift = new_max + jnp.where(seen[b], 0.0, -LOW)
            weights.append(jnp.exp2(pieces[b] - shift).astype(jnp.bfloat16))
        return new_max, jnp.concatenate(weights, axis=0)

    def finish(head, new_max, weights):
        values = jnp.concatenate([columns(ref, kv_heads + head) for ref in blocks], axis=0)
        product = jnp.dot(
            turned_with_ones(values), weights, preferred_element_type=jnp.float32
        )
        acc, total = product[:HD], product[HD : HD + 1]
        if not first:
            fade = jnp.exp2(stat_in[head, 0:1] - new_max)
            acc += acc_in[head] * fade
            total += stat_in[head, 1:2] * fade
        if not final:
            acc_out[head] = acc
            stat_out[head, 0:1] = new_max
            stat_out[head, 1:2] = total
            return
        result = (acc * (1.0 / total)).astype(jnp.bfloat16)
        for h in range(group):
            out_ref[:, lanes(head * group + h)] = (
                result[:, h * rows : (h + 1) * rows].T
            )

    def incoming(head):
        return jnp.concatenate(
            [pages_here(ref, head, kv_heads, own, rows, lanes) for ref in blocks], axis=0
        )

    def decode(head):
        all_pages = jnp.concatenate([ref[head] for ref in pages] + [incoming(head)], axis=0)
        decode_rows = decode_ref.shape[0]
        queries = jnp.concatenate(
            [decode_ref[:, lanes(head * group + h)] for h in range(group)], axis=0
        )
        side_max = side_stat[head, 0:1]
        new_max, product = counted_piece(
            queries,
            all_pages[:, :HD],
            turned_with_ones(all_pages[:, HD:]),
            1.0,
            bias_ref[...],
            side_max,
        )
        fade = jnp.exp2(side_max - new_max)
        acc = product[:HD] + side_acc[head] * fade
        total = product[HD : HD + 1] + side_stat[head, 1:2] * fade
        result = (acc / total).T.astype(jnp.bfloat16)
        for h in range(group):
            decode_out[:, lanes(head * group + h)] = result[h * decode_rows : (h + 1) * decode_rows]

    scores, waiting = score(first_head), None
    for index in range(unroll):
        head = first_head + index
        later = score(head + 1) if index + 1 < unroll else None
        ready = weigh(head, scores)
        if waiting is not None:
            finish(head - 1, *waiting)
        if final:
            decode(head)
        else:
            page_out[head] = incoming(head)
        scores, waiting = later, ready
    finish(first_head + unroll - 1, *waiting)


def attend(arrived, section, query, state, decode, kv_heads):
    blocks = [block for block, _ in arrived]
    place = jnp.stack([section] + [s.astype(jnp.int32) for _, s in arrived])
    n_blocks = len(blocks)
    rows, query_width = query.shape
    group = query_width // (kv_heads * HD)
    first, final = state is None, decode is not None
    total_rows = group * rows
    unroll = math.gcd(kv_heads, 2)
    vmem = pl.BlockSpec(memory_space=pltpu.VMEM)
    operands = [query, *blocks]
    held = []
    if not first:
        acc, stats, held = state
        operands += [acc, stats]
    if final:
        operands += [*decode, *held]
        out_shape = (
            jax.ShapeDtypeStruct(query.shape, jnp.bfloat16),
            jax.ShapeDtypeStruct(decode[0].shape, jnp.bfloat16),
        )
    else:
        out_shape = (
            jax.ShapeDtypeStruct((kv_heads, HD, total_rows), jnp.float32),
            jax.ShapeDtypeStruct((kv_heads, 8, total_rows), jnp.float32),
            jax.ShapeDtypeStruct((kv_heads, n_blocks * CAP * PAGE, 2 * HD), jnp.bfloat16),
        )
    pairs = kv_heads * total_rows * n_blocks * rows
    result = pl.pallas_call(
        functools.partial(
            attend_kernel, n_blocks, len(held), kv_heads, group, unroll, first, final
        ),
        out_shape=out_shape,
        grid=(kv_heads // unroll,),
        in_specs=[pl.BlockSpec(memory_space=pltpu.SMEM)] + [vmem] * len(operands),
        out_specs=[vmem] * len(out_shape),
        compiler_params=params(),
        cost_estimate=pl.CostEstimate(
            flops=6 * pairs * HD,
            bytes_accessed=12 * kv_heads * total_rows * HD,
            transcendentals=pairs,
        ),
        name="attend",
    )(place, *operands)
    if final:
        return result
    return result[0], result[1], [*held, result[2]]


def fence(*arrays):
    return lax.optimization_barrier(arrays)


def grid_sections():
    here = lax.axis_index("section")
    z, column = here // 4, here % 4
    inner = (z == 1) | (z == 2)
    plane_a = jnp.bitwise_xor(z, 1)
    plane_f = jnp.where(inner, 3 - z, jnp.where(z == 0, 2, 1))
    plane_g = jnp.where(inner, jnp.bitwise_xor(3 - z, 1), 3 - z)
    order = [(z, 0), (z, 1), (z, 2), (plane_a, 0), (z, 3), (plane_a, 2), (plane_f, 0)]
    order += [(plane_a, 1), (plane_f, 2), (plane_g, 0), (plane_f, 1), (plane_g, 2), (plane_f, 3)]
    order += [(plane_g, 1), (plane_a, 3), (plane_g, 3)]
    return [plane * 4 + jnp.bitwise_xor(column, turn) for plane, turn in order]


def gather_rounds(own, sections, work):
    sections = iter(sections)

    def named(*blocks):
        return [(block, next(sections)) for block in blocks]

    def settle(moved, work, *kept):
        return fence(*moved, *kept, *work)[: len(moved) + len(kept)]

    size_z, size_y, size_x = 4, 2, 2
    z = lax.axis_index("section") // 4

    def index(zz, yy, xx):
        return (zz * size_y + yy) * size_x + xx

    def along_z(pairs):
        return [
            (index(a, yy, xx), index(b, yy, xx))
            for a, b in pairs
            for yy in range(size_y)
            for xx in range(size_x)
        ]

    every = [(zz, yy, xx) for zz in range(size_z) for yy in range(size_y) for xx in range(size_x)]
    swap_x = [(index(zz, yy, xx), index(zz, yy, 1 - xx)) for zz, yy, xx in every]
    swap_y = [(index(zz, yy, xx), index(zz, 1 - yy, xx)) for zz, yy, xx in every]
    ends = along_z([(0, 1), (1, 0), (2, 3), (3, 2)])
    middle = along_z([(1, 2), (2, 1)])
    outward = along_z([(1, 0), (2, 3)])
    inner = (z == 1) | (z == 2)

    def move(block, pairs):
        return lax.ppermute(block, "section", pairs)

    moved = move(own, swap_x), move(own, swap_y), move(own, ends), move(own, middle)
    own_x, own_y, a, b = settle(moved, work)
    work = yield named(own, own_x, own_y, a)
    moved = move(own_y, swap_x), move(a, swap_y), move(b, outward), move(a, middle)
    own_d, a_y, c, d, a, b = settle(moved, work, a, b)
    f = jnp.where(inner, b, c)
    work = yield named(own_d, a_y, f)
    either = jnp.where(inner, d, own_d)
    moved = move(a, swap_x), move(f, swap_y), move(either, ends), move(own_d, middle)
    a_x, f_y, e, b_in, f, d = settle(moved, work, f, d)
    g = jnp.where(inner, d, e)
    work = yield named(a_x, f_y, g)
    moved = move(f, swap_x), move(g, swap_y), move(b_in, outward), move(e, middle)
    f_x, g_y, c_in, d_in, g, a_x, b_in, e = settle(moved, work, g, a_x, b_in, e)
    f_d = jnp.where(inner, b_in, c_in)
    work = yield named(f_x, g_y, f_d)
    moved = move(g, swap_x), move(a_x, swap_y), move(d_in, outward)
    g_x, a_turn, e_in = settle(moved, work)
    a_d = jnp.where(inner, e, a_turn)
    g_d = jnp.where(inner, d_in, e_in)
    yield named(g_x, a_d, g_d)


def plain_sections(section_count, section, pool):
    every = [jnp.int32(s) for s in range(section_count)]
    return [jnp.where(s == section, -pool, s) for s in every]


def gather_plain(own, section_count):
    rows = own.shape[0]
    gathered = lax.all_gather(own, "section", axis=0, tiled=True)
    step = math.gcd(section_count, 4)
    for top in range(0, section_count, step):
        yield [
            (gathered[s * rows : (s + 1) * rows], jnp.int32(s)) for s in range(top, top + step)
        ]


def per_device(
    prefill_hidden,
    norm_gain,
    key_weight,
    value_weight,
    prefill_query,
    resident_keys,
    resident_values,
    decode_query,
    page_owner,
    block_table,
    context_len,
):
    section_count = lax.axis_size("section")
    tp_count = lax.axis_size("tp")
    section = lax.axis_index("section").astype(jnp.int32)
    tp = lax.axis_index("tp").astype(jnp.int32)
    rows = prefill_hidden.shape[0]
    key_width = key_weight.shape[1]
    kv_heads = key_width // HD
    group = prefill_query.shape[1] // key_width
    pool = resident_keys.shape[0]

    if tp_count == 2:
        other = lax.ppermute(prefill_hidden, "tp", [(0, 1), (1, 0)])
        parts, order = [prefill_hidden, other], jnp.stack([tp, 1 - tp])
    else:
        parts = [lax.all_gather(prefill_hidden, "tp", axis=1, tiled=True)]
        order = jnp.zeros((1,), jnp.int32)
    half = HD // 2
    frequency = jnp.exp(jnp.arange(half, dtype=jnp.float32) * (-2.0 * math.log(ROPE_THETA) / HD))
    positions = section * rows + jnp.arange(rows, dtype=jnp.int32)
    angles = positions.astype(jnp.float32)[:, None] * frequency[None, :]
    cosine, sine = jnp.cos(angles), jnp.sin(angles)
    cosine = EXP2_SCALE * jnp.concatenate([cosine, cosine], axis=1)
    sine = EXP2_SCALE * jnp.concatenate([-sine, sine], axis=1)

    key_near, value_near = stage(key_weight, value_weight)
    own = project(
        parts, order, norm_gain, key_near, value_near, cosine, sine, page_owner
    )

    own, block_table, context_len = fence(own, block_table, context_len)
    table = jnp.concatenate([block_table] * group, axis=0).T
    lengths = jnp.concatenate([context_len] * group)[None, :]
    if section_count == 16:
        sections = grid_sections()
    else:
        sections = [section] + plain_sections(section_count, section, pool)
    decode = (
        decode_query,
        *resident_attention(
            decode_query,
            resident_keys.reshape(pool * PAGE, key_width),
            resident_values.reshape(pool * PAGE, key_width),
            table,
            lengths,
            jnp.stack(sections).astype(jnp.int32),
            pool,
        ),
    )

    def step(arrived, state, last=False):
        return attend(arrived, section, prefill_query, state, decode if last else None, kv_heads)

    if section_count == 16:
        rounds = gather_rounds(own, sections, decode[1:])
        arrived, state = next(rounds), None
        for _ in range(4):
            state = step(arrived, state)
            arrived = rounds.send((state[0], state[1]))
        return step(arrived, state, True)
    state = step([(own, section)], None)
    rounds = list(gather_plain(own, section_count))
    for arrived in rounds[:-1]:
        state = step(arrived, state)
    return step(rounds[-1], state, True)


def solution(mesh):
    return jax.shard_map(
        per_device,
        mesh=mesh,
        in_specs=(
            P("section", "tp"),
            P(),
            P(None, "tp"),
            P(None, "tp"),
            P("section", "tp"),
            P("section", None, "tp"),
            P("section", None, "tp"),
            P("section", "tp"),
            P("section"),
            P("section", None),
            P("section"),
        ),
        out_specs=(P("section", "tp"), P("section", "tp")),
        check_vma=False,
    )
```
